256 devices in a mesh: gx: 8 (over x, core), gy: 32 (over z, y).
Axes of the slice: x: 4, y: 4, z: 8, core: 2. Of those that a mesh axis runs over, the one named last changes fastest.
Arguments:
- multipoles: float32 [165, 524288], P(None, ('gx', 'gy')), may hold values from -6 to 6
- coarse_poles: float32 [165, 16384], P(None, ('gx', 'gy')), may hold values from -6 to 6
- operators: float32 [32, 165, 165], replicated, may hold values from -0.078125 to 0.078125
- block_lists: int32 [8192, 32], P(('gx', 'gy')), may hold values from -1 to 159, as said below
- coarse_lists: int32 [16384, 32], P(('gx', 'gy')), may hold values from -1 to 16383, as said below
- send_lists: int32 [256, 8, 16], P(('gx', 'gy')), may hold values from 0 to 143, as said below
- live_blocks: int32 [256], P(('gx', 'gy')), may hold values from 1 to 32
Outputs:
- fine_local: float32 [165, 524288], P(None, ('gx', 'gy'))
- coarse_local: float32 [165, 16384], P(None, ('gx', 'gy'))
The draws below stay inside these ranges and needn't reach their ends.
Inputs may be any that keep to these rules, and one draw needn't show every extreme that they name: `send_lists`: at bit k, an entry indexes the 32 + k * 16 blocks held before that step. `block_lists`: -1 marks an empty slot. `coarse_lists`: -1 marks an empty slot.
All inputs are finite; a program needn't handle non-finite values.
Results may differ from the reference program's by a relative error of at most 0.0001.
Values sent between devices are 32-bit elements; how exact they have to be, the bound alone decides.
A program may use at most 192 MiB of HBM per device.

```python
import jax
import jax.numpy as jnp
import numpy as np
from jax import lax

COEF = 165
BCELLS = 64
NL = 32
BLK_DEV = 32
SEND = 16
BITS = 8
LET_BLK = 160
TBLK = 8192
CELLS = 524288
COARSE = 16384
N_GX = 8
N_GY = 32


def draw_send_lists(key, part):
    key = jax.random.fold_in(key, 11)
    tops = BLK_DEV + SEND * jnp.arange(BITS, dtype=jnp.int32)
    raw = jax.random.randint(key, (N_GX * N_GY, BITS, SEND), 0, 1 << 20, dtype=jnp.int32)
    values = raw % tops[None, :, None]
    values = values.at[0, BITS - 1, 0].set(BLK_DEV + (BITS - 1) * SEND - 1)
    values = values.at[0, 0, 0].set(0)
    return values.astype(jnp.int32)


def draw_block_lists(key, part):
    key = jax.random.fold_in(key, 23)
    first, second = jax.random.split(key)
    values = jax.random.randint(first, (TBLK, NL), 0, LET_BLK, dtype=jnp.int32)
    holes = jax.random.randint(second, (TBLK, NL), 0, 8, dtype=jnp.int32)
    values = jnp.where(holes == 0, -1, values)
    values = values.at[0, 0].set(LET_BLK - 1)
    values = values.at[0, 1].set(-1)
    return values.astype(jnp.int32)


def draw_coarse_lists(key, part):
    key = jax.random.fold_in(key, 37)
    first, second = jax.random.split(key)
    values = jax.random.randint(first, (COARSE, NL), 0, COARSE, dtype=jnp.int32)
    holes = jax.random.randint(second, (COARSE, NL), 0, 8, dtype=jnp.int32)
    values = jnp.where(holes == 0, -1, values)
    values = values.at[0, 0].set(COARSE - 1)
    values = values.at[0, 1].set(-1)
    return values.astype(jnp.int32)


def draw_live_blocks(key, part):
    key = jax.random.fold_in(key, 41)
    values = jax.random.randint(key, (N_GX * N_GY,), 1, BLK_DEV + 1, dtype=jnp.int32)
    values = values.at[0].set(BLK_DEV)
    values = values.at[1].set(1)
    return values.astype(jnp.int32)


def shard_levels(own_key, extent, cuts, smallest, high):
    loudness = 1.0
    for axis_at, parts in cuts:
        steps = jax.random.uniform(jax.random.fold_in(jax.random.fold_in(own_key, 6), axis_at), (parts,), jnp.float32, smallest / len(cuts), high / len(cuts))
        loudness = loudness * jnp.repeat(jnp.exp(steps), extent[axis_at] // parts).reshape((-1,) + (1,) * (len(extent) - 1 - axis_at))
    return loudness


def bell_draw(own_key, extent, deviation, reach, pieces=(), kind=jnp.bfloat16):
    values = jax.random.normal(own_key, extent, jnp.float32) * deviation
    if len(pieces) > 0:
        values = shard_levels(own_key, extent, pieces, -0.22, 0.18) * values
    return jnp.clip(values, min=-reach, max=reach).astype(kind)


def setup_inputs(seed: int = 0) -> dict:
    key_list = jax.random.split(jax.random.key(seed), 8)
    multipoles = bell_draw(key_list[0], (COEF, CELLS), 1.0, 6.0, ((1, 256),), jnp.float32)
    coarse_poles = bell_draw(key_list[1], (COEF, COARSE), 1.0, 6.0, ((1, 256),), jnp.float32)
    operators = bell_draw(key_list[2], (NL, COEF, COEF), (COEF * NL) ** -0.5, 0.078125, (), jnp.float32)
    block_lists = draw_block_lists(jax.random.fold_in(key_list[7], 71), 0)
    coarse_lists = draw_coarse_lists(jax.random.fold_in(key_list[7], 71), 0)
    send_lists = draw_send_lists(jax.random.fold_in(key_list[7], 71), 0)
    live_blocks = draw_live_blocks(jax.random.fold_in(key_list[7], 71), 0)
    return {"multipoles": multipoles, "coarse_poles": coarse_poles, "operators": operators, "block_lists": block_lists, "coarse_lists": coarse_lists, "send_lists": send_lists, "live_blocks": live_blocks}


def reference(multipoles, coarse_poles, operators, block_lists, coarse_lists, send_lists, live_blocks):
    ndev = N_GX * N_GY
    blocks = multipoles.reshape(COEF, ndev, BLK_DEV, BCELLS).transpose(1, 0, 2, 3)
    for step in range(BITS):
        partner = np.arange(ndev) ^ (1 << step)
        index = send_lists[:, step, :].astype(jnp.int32)
        outgoing = jnp.take_along_axis(blocks, index[:, None, :, None], axis=2)
        blocks = jnp.concatenate([blocks, outgoing[partner]], axis=2)
    empty = jnp.zeros((ndev, COEF, 1, BCELLS), blocks.dtype)
    blocks = jnp.concatenate([blocks, empty], axis=2)
    table = blocks.transpose(1, 0, 2, 3).reshape(COEF, ndev * (LET_BLK + 1), BCELLS)
    owner = (jnp.arange(TBLK, dtype=jnp.int32) // BLK_DEV) * (LET_BLK + 1)
    local = jnp.where(block_lists < 0, LET_BLK, block_lists).astype(jnp.int32)
    global_index = (owner[:, None] + local).astype(jnp.int32)

    def fine_slot(total, pair):
        op, column = pair
        source = jnp.take(table, column, axis=1).reshape(COEF, CELLS)
        return total + jnp.dot(op, source, precision=lax.Precision.HIGHEST, preferred_element_type=jnp.float32), None

    fine_raw, _ = lax.scan(fine_slot, jnp.zeros((COEF, CELLS), multipoles.dtype), (operators, global_index.T))
    position = jnp.arange(TBLK, dtype=jnp.int32)
    bounds = live_blocks[position // BLK_DEV]
    inside = jnp.repeat((position % BLK_DEV) < bounds, BCELLS)
    fine_local = jnp.where(inside[None, :], fine_raw, jnp.zeros_like(fine_raw))

    extended = jnp.concatenate([coarse_poles, jnp.zeros((COEF, 1), coarse_poles.dtype)], axis=1)
    coarse_index = jnp.where(coarse_lists < 0, COARSE, coarse_lists).astype(jnp.int32)

    def coarse_slot(total, pair):
        op, column = pair
        source = jnp.take(extended, column, axis=1)
        return total + jnp.dot(op, source, precision=lax.Precision.HIGHEST, preferred_element_type=jnp.float32), None

    coarse_local, _ = lax.scan(coarse_slot, jnp.zeros((COEF, COARSE), coarse_poles.dtype), (operators, coarse_index.T))
    return fine_local, coarse_local
```

```python
import functools
import jax
import jax.numpy as jnp
from jax import lax
from jax.experimental import pallas as pl
from jax.experimental.pallas import tpu as pltpu
from jax.sharding import PartitionSpec as P

BCELLS = 64
ROWS = 16
MESH = pl.DeviceIdType.MESH


def coarse_terms(operators, everything, coarse_lists):
    coef_rows = everything.shape[1]
    count = everything.shape[0]
    extended = jnp.concatenate([everything, jnp.zeros((1, coef_rows), everything.dtype)], axis=0)
    safe = jnp.where(coarse_lists < 0, count, coarse_lists)
    taken = jnp.take(extended, safe.T.reshape(-1), axis=0).reshape(
        operators.shape[0], -1, coef_rows
    )
    return jnp.einsum(
        "jcd,jtd->ct",
        operators,
        taken,
        precision=lax.Precision.HIGH,
        preferred_element_type=jnp.float32,
    )


def lanes_below(shape, limit):
    return lax.broadcasted_iota(jnp.int32, shape, len(shape) - 1) < limit


def fine_kernel(
    groups, steps, own, sent, low_bits, offsets,
    mult_ref, ops_ref, send_ref, lists_ref, live_ref,
    out_ref,
    table, outgo, landed, split, mats, total, send_sem, recv_sem,
):
    slots, coef, _ = ops_ref.shape
    gx = lax.axis_index("gx")
    gy = lax.axis_index("gy")

    def partner(k):
        if k < low_bits:
            bit = 1 << k
            up = lax.rem(gy // bit, 2)
            return (gx, gy + bit - 2 * bit * up)
        bit = 1 << (k - low_bits)
        up = lax.rem(gx // bit, 2)
        return (gx + bit - 2 * bit * up, gy)

    def copy(g, k):
        return pltpu.make_async_remote_copy(
            src_ref=outgo.at[g, k],
            dst_ref=landed.at[g, k],
            send_sem=send_sem.at[g, k],
            recv_sem=recv_sem.at[g, k],
            device_id=partner(k),
            device_id_type=MESH,
        )

    barrier = pltpu.get_barrier_semaphore()
    for k in range(steps):
        pl.semaphore_signal(barrier, inc=1, device_id=partner(k), device_id_type=MESH)

    half = lanes_below((8, 128), 64)

    def own_blocks(g, carry):
        def pair(p, c):
            lanes = pl.ds(pl.multiple_of(p * 128, 128), 128)
            first = mult_ref[pl.ds(pl.multiple_of(g * ROWS, 8), 8), lanes]
            second = mult_ref[pl.ds(pl.multiple_of(g * ROWS + 8, 8), 8), lanes]
            table[g, 2 * p] = jnp.where(half, first, pltpu.roll(second, 64, 1))
            table[g, 2 * p + 1] = jnp.where(half, pltpu.roll(first, 64, 1), second)
            return c

        return lax.fori_loop(0, own // 2, pair, carry, unroll=True)

    lax.fori_loop(0, groups, own_blocks, 0)
    split[0] = jnp.zeros((ROWS, 128), jnp.bfloat16)
    pl.semaphore_wait(barrier, steps)

    def send(g, k):
        if k > 0:
            copy(g, k - 1).wait_recv()
            first = own + (k - 1) * sent
            table[g, first : first + sent] = landed[g, k - 1]
        for i in range(sent):
            outgo[g, k, i] = table[g, send_ref[k, i]]
        copy(g, k).start()

    def arrange(q):
        per = 128 // ROWS
        lane = lax.broadcasted_iota(jnp.int32, (ROWS, 128), 1)
        tail = coef - 128

        def rows_at(read, at):
            tiles = []
            for i in range(per):
                full = read(q * per + i)
                tiles.append(
                    (
                        full[:, :128],
                        jnp.concatenate(
                            [full[:, 128:], jnp.zeros((ROWS, 128 - tail), jnp.float32)], axis=1
                        ),
                    )
                )
            for g in range(groups):
                which, at_lane = divmod(g * ROWS, 128)
                value = jnp.zeros((ROWS, 128), jnp.float32)
                for i in range(per):
                    shift = (i * ROWS - at_lane) % 128
                    piece = tiles[i][which]
                    if shift:
                        piece = pltpu.roll(piece, shift, 1)
                    value = jnp.where((lane >= i * ROWS) & (lane < (i + 1) * ROWS), piece, value)
                high = value.astype(jnp.bfloat16)
                low = (value - high.astype(jnp.float32)).astype(jnp.bfloat16)
                height = mats.shape[1] // 2
                mats[g, pl.ds(at, ROWS), pl.ds(pl.multiple_of(q * 128, 128), 128)] = high
                mats[g, pl.ds(height + at, ROWS), pl.ds(pl.multiple_of(q * 128, 128), 128)] = low

        whole = coef // ROWS

        def body(r, c):
            at = pl.multiple_of(r * ROWS, ROWS)
            rows_at(lambda j: ops_ref[j, pl.ds(at, ROWS), :], at)
            return c

        lax.fori_loop(0, whole, body, 0)
        left = coef - whole * ROWS
        rows_at(
            lambda j: jnp.concatenate(
                [
                    ops_ref[j, whole * ROWS : coef, :],
                    jnp.zeros((ROWS - left, coef), jnp.float32),
                ],
                axis=0,
            ),
            whole * ROWS,
        )

    def multiply(g):
        copy(g, steps - 1).wait_recv()
        first = own + (steps - 1) * sent
        table[g, first : first + sent] = landed[g, steps - 1]
        halves = lanes_below((16, 8, 128), 64)

        def cut(c, carry):
            at = pl.multiple_of(c * 16, 16)
            block = table[g, pl.ds(at, 16)]
            high = block.astype(jnp.bfloat16).astype(jnp.float32)
            low = block - high
            top = jnp.where(halves, high, pltpu.roll(low, 64, 2))
            bottom = jnp.where(halves, pltpu.roll(high, 64, 2), low)
            split[pl.ds(at + 1, 16)] = jnp.concatenate([top, bottom], axis=1).astype(jnp.bfloat16)
            return carry

        lax.fori_loop(0, (own + steps * sent) // 16, cut, 0)
        height = mats.shape[1] // 2

        def targets(p, carry):
            sides = []
            for side in range(2):
                sides.append(
                    jnp.concatenate(
                        [split[lists_ref[2 * p + side, j] + 1] for j in range(slots)], axis=0
                    )
                )
            source = jnp.concatenate(sides, axis=1)
            product = jnp.dot(mats[g], source, preferred_element_type=jnp.float32)
            lanes = pl.ds(pl.multiple_of(p * 256, 256), 256)
            total[:, lanes] += product[:height] + product[height:]
            return carry

        lax.fori_loop(0, own // 2, targets, 0)

    total[...] = jnp.zeros_like(total)

    def tick(s, carry):
        for k in reversed(range(steps)):
            g = s - offsets[k]

            @pl.when((g >= 0) & (g < groups))
            def _():
                send(g, k)

        @pl.when(s < slots * ROWS // 128)
        def _():
            arrange(s)

        g = s - offsets[steps]

        @pl.when((g >= 0) & (g < groups))
        def _():
            multiply(g)

        return carry

    lax.fori_loop(0, groups + offsets[steps], tick, 0)

    def drain(g, carry):
        for k in range(steps):
            copy(g, k).wait_send()
        return carry

    lax.fori_loop(0, groups, drain, 0)

    live = live_ref[0]
    side = lanes_below((coef, 128), 64)

    def finish(p, carry):
        left = total[:coef, pl.ds(pl.multiple_of(p * 256, 256), 128)]
        right = total[:coef, pl.ds(pl.multiple_of(p * 256 + 128, 128), 128)]
        left = left + pltpu.roll(left, 64, 1)
        right = right + pltpu.roll(right, 64, 1)
        both = jnp.where(side, left, right)
        position = 2 * p + jnp.where(side, 0, 1)
        out_ref[:, pl.ds(pl.multiple_of(p * 128, 128), 128)] = jnp.where(position < live, both, 0.0)
        return carry

    lax.fori_loop(0, own // 2, finish, 0)


def fine_part(multipoles, operators, block_lists, send_lists, live_blocks):
    coef, cells = multipoles.shape
    slots = operators.shape[0]
    own = cells // BCELLS
    _, steps, sent = send_lists.shape
    groups = -(-coef // ROWS)
    low_bits = lax.axis_size("gy").bit_length() - 1
    offsets = tuple(range(steps + 1))
    padded = jnp.pad(multipoles, ((0, groups * ROWS - coef), (0, 0)))
    vmem = pl.BlockSpec(memory_space=pltpu.VMEM)
    smem = pl.BlockSpec(memory_space=pltpu.SMEM)
    return pl.pallas_call(
        functools.partial(fine_kernel, groups, steps, own, sent, low_bits, offsets),
        out_shape=jax.ShapeDtypeStruct((coef, cells), jnp.float32),
        in_specs=[vmem, vmem, smem, smem, smem],
        out_specs=vmem,
        scratch_shapes=[
            pltpu.VMEM((groups, own + steps * sent, 8, 128), jnp.float32),
            pltpu.VMEM((groups, steps, sent, 8, 128), jnp.float32),
            pltpu.VMEM((groups, steps, sent, 8, 128), jnp.float32),
            pltpu.VMEM((own + steps * sent + 1, ROWS, 128), jnp.bfloat16),
            pltpu.VMEM((groups, 2 * groups * ROWS, slots * ROWS), jnp.bfloat16),
            pltpu.VMEM((groups * ROWS, own * 128), jnp.float32),
            pltpu.SemaphoreType.DMA((groups, steps)),
            pltpu.SemaphoreType.DMA((groups, steps)),
        ],
        compiler_params=pltpu.CompilerParams(
            collective_id=0, has_side_effects=True, vmem_limit_bytes=60 << 20
        ),
        cost_estimate=pl.CostEstimate(
            flops=8 * slots * coef * coef * cells, bytes_accessed=8 << 20, transcendentals=0
        ),
        name="fine",
    )(padded, operators, send_lists[0], block_lists, live_blocks)


def shards(multipoles, coarse_poles, operators, block_lists, coarse_lists, send_lists, live_blocks):
    everything = lax.all_gather(coarse_poles.T, ("gx", "gy"), axis=0, tiled=True)
    fine_local = fine_part(multipoles, operators, block_lists, send_lists, live_blocks)
    coarse_local = coarse_terms(operators, everything, coarse_lists)
    return (fine_local, coarse_local)


def solution(mesh):
    return jax.shard_map(
        shards,
        mesh=mesh,
        in_specs=(
            P(None, ("gx", "gy")),
            P(None, ("gx", "gy")),
            P(),
            P(("gx", "gy"), None),
            P(("gx", "gy"), None),
            P(("gx", "gy"), None, None),
            P(("gx", "gy")),
        ),
        out_specs=(P(None, ("gx", "gy")), P(None, ("gx", "gy"))),
        check_vma=False,
    )
```

```python
import functools
import jax
import jax.numpy as jnp
from jax import lax
from jax.experimental import pallas as pl
from jax.experimental.pallas import tpu as pltpu
from jax.sharding import PartitionSpec as P

BCELLS = 64
ROWS = 16
XCHIPS = 4
WIDTH = 42
PARTS = 3
PACKED = 24
CHUNK = 4
Y_TICK = 3
CORE_TICK = 8
ARRANGE_TICK = 4
COARSE_TICK = 11
MESH = pl.DeviceIdType.MESH


def lanes_below(shape, limit):
    return lax.broadcasted_iota(jnp.int32, shape, len(shape) - 1) < limit


def fine_kernel(
    groups, steps, own, sent, low_bits, offsets,
    mult_ref, coarse_ref, ops_hbm, codes_ref, send_ref, lists_ref, live_ref,
    out_ref, coarse_out_ref,
    table, outgo, landed, split, mats, total, ops_ref,
    packed, everything, codes, codes_smem, replicas, gathered, partial, incoming,
    send_sem, recv_sem, ops_sem, slice_send, slice_recv, code_send, code_recv,
    z_send, z_recv, y_send, y_recv, core_send, core_recv, sum_send, sum_recv, smem_sem,
):
    slots, coef, _ = ops_ref.shape
    gx = lax.axis_index("gx")
    gy = lax.axis_index("gy")
    chip, core = gx // 2, lax.rem(gx, 2)
    z, y = gy // 4, lax.rem(gy, 4)
    cells = coarse_ref.shape[0]

    def x_peer(o):
        return lax.rem(chip + o, XCHIPS)

    def x_device(o):
        return (x_peer(o) * 2 + core, gy)

    def z_device(o):
        return (gx, lax.rem(z + o, 8) * 4 + y)

    def y_device(o):
        return (gx, z * 4 + lax.rem(y + o, 4))

    def core_device():
        return (gx + 1 - 2 * core, gy)

    def rows_of(c, yy, zz, xx, count):
        at = (((c * 4 + yy) * 8 + zz) * XCHIPS + xx) * PACKED
        return pl.ds(pl.multiple_of(at, 8), count * PACKED)

    def remote(source, target, send, recv, device):
        return pltpu.make_async_remote_copy(
            src_ref=source, dst_ref=target, send_sem=send, recv_sem=recv,
            device_id=device, device_id_type=MESH,
        )

    def slice_copy(o):
        return remote(
            packed.at[x_peer(o)], everything.at[rows_of(core, y, z, chip, 1)],
            slice_send.at[o - 1], slice_recv.at[o - 1], x_device(o),
        )

    def code_copy(o):
        return remote(
            codes_ref, codes.at[chip], code_send.at[o - 1], code_recv.at[o - 1], x_device(o)
        )

    def z_copy(o):
        rows = rows_of(core, y, z, 0, XCHIPS)
        return remote(
            everything.at[rows], everything.at[rows], z_send.at[o - 1], z_recv.at[o - 1], z_device(o)
        )

    def y_copy(o):
        rows = rows_of(core, y, 0, 0, 8 * XCHIPS)
        return remote(
            everything.at[rows], everything.at[rows], y_send.at[o - 1], y_recv.at[o - 1], y_device(o)
        )

    def core_copy():
        rows = rows_of(core, 0, 0, 0, 32 * XCHIPS)
        return remote(everything.at[rows], everything.at[rows], core_send, core_recv, core_device())

    def sum_copy(o):
        return remote(
            partial.at[x_peer(o)], incoming.at[chip],
            sum_send.at[o - 1], sum_recv.at[o - 1], x_device(o),
        )

    def ops_copy(j):
        return pltpu.make_async_copy(ops_hbm.at[:, j, :], ops_ref.at[j], ops_sem.at[j])

    def codes_copy():
        return pltpu.make_async_copy(codes.at[:, 0:slots], codes_smem, smem_sem)

    def partner(k):
        if k < low_bits:
            bit = 1 << k
            up = lax.rem(gy // bit, 2)
            return (gx, gy + bit - 2 * bit * up)
        bit = 1 << (k - low_bits)
        up = lax.rem(gx // bit, 2)
        return (gx + bit - 2 * bit * up, gy)

    def copy(g, k):
        return pltpu.make_async_remote_copy(
            src_ref=outgo.at[g, k],
            dst_ref=landed.at[g, k],
            send_sem=send_sem.at[g, k],
            recv_sem=recv_sem.at[g, k],
            device_id=partner(k),
            device_id_type=MESH,
        )

    barrier = pltpu.get_barrier_semaphore()
    peers = [x_device(o) for o in range(1, XCHIPS)] + [z_device(o) for o in range(1, 8)]
    peers += [y_device(o) for o in range(1, 4)] + [core_device()]
    for peer in peers:
        pl.semaphore_signal(barrier, inc=1, device_id=peer, device_id_type=MESH)
    lax.fori_loop(0, slots, lambda j, c: (ops_copy(j).start(), c)[1], 0)

    lane64 = lax.broadcasted_iota(jnp.int32, (cells, 128), 1)
    near = coarse_ref[:, :128]
    far = jnp.concatenate(
        [coarse_ref[:, 128:], jnp.zeros((cells, 256 - coef), jnp.float32)], axis=1
    )
    for x in range(XCHIPS):
        shift = (128 - WIDTH * x) % 128
        base = pltpu.roll(near, shift, 1) if shift else near
        if x == XCHIPS - 1:
            base = jnp.where(lane64 < shift, base, pltpu.roll(far, shift, 1))
        base = jnp.where(lane64 < WIDTH, base, 0.0)
        rest = jnp.concatenate(
            [base[2 * PACKED :], jnp.zeros((3 * PACKED - cells, 128), jnp.float32)], axis=0
        )
        packed[x] = (
            base[:PACKED]
            + pltpu.roll(base[PACKED : 2 * PACKED], WIDTH, 1)
            + pltpu.roll(rest, 2 * WIDTH, 1)
        )
    everything[rows_of(core, y, z, chip, 1)] = packed[chip]
    codes[chip] = codes_ref[...]

    half = lanes_below((8, 128), 64)

    def place(g, p, first, second):
        table[g, 2 * p] = jnp.where(half, first, pltpu.roll(second, 64, 1))
        table[g, 2 * p + 1] = jnp.where(half, pltpu.roll(first, 64, 1), second)

    def own_blocks(g):
        def pair(p, c):
            lanes = pl.ds(pl.multiple_of(p * 128, 128), 128)
            first = mult_ref[pl.ds(pl.multiple_of(g * ROWS, 8), 8), lanes]
            second = mult_ref[pl.ds(pl.multiple_of(g * ROWS + 8, 8), 8), lanes]
            place(g, p, first, second)
            return c

        lax.fori_loop(0, own // 2, pair, 0, unroll=True)

    def last_blocks():
        g = groups - 1
        left = coef - g * ROWS

        def pair(p, c):
            lanes = pl.ds(pl.multiple_of(p * 128, 128), 128)
            first = jnp.concatenate(
                [mult_ref[g * ROWS : coef, lanes], jnp.zeros((8 - left, 128), jnp.float32)], axis=0
            )
            place(g, p, first, jnp.zeros((8, 128), jnp.float32))
            return c

        lax.fori_loop(0, own // 2, pair, 0)

    own_blocks(0)
    split[0] = jnp.zeros((ROWS, 128), jnp.bfloat16)
    pl.semaphore_wait(barrier, len(peers))

    def send(g, k):
        if k > 0:
            copy(g, k - 1).wait_recv()
            first = own + (k - 1) * sent
            table[g, first : first + sent] = landed[g, k - 1]
        for i in range(sent):
            outgo[g, k, i] = table[g, send_ref[k, i]]
        copy(g, k).start()

    def arrange(q):
        per = 128 // ROWS
        lane = lax.broadcasted_iota(jnp.int32, (ROWS, 128), 1)
        tail = coef - 128
        beyond = (lane >= 2) & (jnp.full((ROWS, 128), chip, jnp.int32) == XCHIPS - 1)
        for i in range(per):
            ops_copy(q * per + i).wait()

        def rows_at(read, at):
            tiles = []
            for i in range(per):
                full = read(q * per + i)
                tiles.append(
                    (
                        full[:, :128],
                        jnp.concatenate(
                            [full[:, 128:], jnp.zeros((ROWS, 128 - tail), jnp.float32)], axis=1
                        ),
                    )
                )
            height = mats.shape[1] // 2
            for i in range(per):
                base = pltpu.roll(tiles[i][0], lax.rem(128 - WIDTH * chip, 128), 1)
                base = jnp.where(beyond, pltpu.roll(tiles[i][1], 2, 1), base)
                base = jnp.where(lane < WIDTH, base, 0.0)
                base = base + pltpu.roll(base, WIDTH, 1) + pltpu.roll(base, 2 * WIDTH, 1)
                high = base.astype(jnp.bfloat16)
                low = (base - high.astype(jnp.float32)).astype(jnp.bfloat16)
                lanes = pl.ds(pl.multiple_of((q * per + i) * 128, 128), 128)
                replicas[pl.ds(at, ROWS), lanes] = high
                replicas[pl.ds(height + at, ROWS), lanes] = low
            for g in range(groups):
                which, at_lane = divmod(g * ROWS, 128)
                value = jnp.zeros((ROWS, 128), jnp.float32)
                for i in range(per):
                    shift = (i * ROWS - at_lane) % 128
                    piece = tiles[i][which]
                    if shift:
                        piece = pltpu.roll(piece, shift, 1)
                    value = jnp.where((lane >= i * ROWS) & (lane < (i + 1) * ROWS), piece, value)
                high = value.astype(jnp.bfloat16)
                low = (value - high.astype(jnp.float32)).astype(jnp.bfloat16)
                mats[g, pl.ds(at, ROWS), pl.ds(pl.multiple_of(q * 128, 128), 128)] = high
                mats[g, pl.ds(height + at, ROWS), pl.ds(pl.multiple_of(q * 128, 128), 128)] = low

        whole = coef // ROWS

        def body(r, c):
            at = pl.multiple_of(r * ROWS, ROWS)
            rows_at(lambda j: ops_ref[j, pl.ds(at, ROWS), :], at)
            return c

        lax.fori_loop(0, whole, body, 0)
        left = coef - whole * ROWS
        rows_at(
            lambda j: jnp.concatenate(
                [
                    ops_ref[j, whole * ROWS : coef, :],
                    jnp.zeros((ROWS - left, coef), jnp.float32),
                ],
                axis=0,
            ),
            whole * ROWS,
        )

    def multiply(g):
        copy(g, steps - 1).wait_recv()
        first = own + (steps - 1) * sent
        table[g, first : first + sent] = landed[g, steps - 1]
        halves = lanes_below((16, 8, 128), 64)

        def cut(c, carry):
            at = pl.multiple_of(c * 16, 16)
            block = table[g, pl.ds(at, 16)]
            high = block.astype(jnp.bfloat16).astype(jnp.float32)
            low = block - high
            top = jnp.where(halves, high, pltpu.roll(low, 64, 2))
            bottom = jnp.where(halves, pltpu.roll(high, 64, 2), low)
            split[pl.ds(at + 1, 16)] = jnp.concatenate([top, bottom], axis=1).astype(jnp.bfloat16)
            return carry

        lax.fori_loop(0, (own + steps * sent) // 16, cut, 0)
        height = mats.shape[1] // 2

        def targets(p, carry):
            sides = []
            for side in range(2):
                sides.append(
                    jnp.concatenate(
                        [split[lists_ref[2 * p + side, j] + 1] for j in range(slots)], axis=0
                    )
                )
            source = jnp.concatenate(sides, axis=1)
            product = jnp.dot(mats[g], source, preferred_element_type=jnp.float32)
            lanes = pl.ds(pl.multiple_of(p * 256, 256), 256)
            total[:, lanes] += product[:height] + product[height:]
            return carry

        lax.fori_loop(0, own // 2, targets, 0)

    lane = lax.broadcasted_iota(jnp.int32, (cells, 128), 1)
    part_of = jnp.where(lane < WIDTH, 0, jnp.where(lane < 2 * WIDTH, 1, jnp.where(lane < 3 * WIDTH, 2, 7)))

    def coarse_chunk(c):
        for i in range(CHUNK):
            def take(n, carry):
                x, first = n // (cells // 16), lax.rem(n, cells // 16) * 16
                for r in range(16):
                    code = codes_smem[x, c * CHUNK + i, first + r]
                    gathered[i, pl.ds(n * 16 + r, 1), :] = everything[
                        pl.ds(lax.shift_right_logical(code, 2), 1), :
                    ]
                return carry

            lax.fori_loop(0, XCHIPS * cells // 16, take, 0)
        highs, lows = [], []
        for x in range(XCHIPS):
            turned = pltpu.roll(codes[x, slots : slots + cells, :], lax.rem(128 - c * CHUNK, 128), 1)
            row_high, row_low = [], []
            for i in range(CHUNK):
                value = gathered[i, x * cells : (x + 1) * cells]
                value = jnp.where(part_of == (turned[:, i : i + 1] & 3), value, 0.0)
                high = value.astype(jnp.bfloat16)
                row_high.append(high)
                row_low.append((value - high.astype(jnp.float32)).astype(jnp.bfloat16))
            highs.append(jnp.concatenate(row_high, axis=1))
            lows.append(jnp.concatenate(row_low, axis=1))
        high = jnp.concatenate(highs, axis=0)
        low = jnp.concatenate(lows, axis=0)
        height = mats.shape[1] // 2
        lanes = pl.ds(pl.multiple_of(c * CHUNK * 128, CHUNK * 128), CHUNK * 128)
        op_high = replicas[:height, lanes]
        op_low = replicas[height:, lanes]
        dims = (((1,), (1,)), ((), ()))

        def dot(a, b):
            return lax.dot_general(a, b, dims, preferred_element_type=jnp.float32)

        product = dot(high, op_high) + dot(low, op_high) + dot(high, op_low)
        for x in range(XCHIPS):
            partial[x] += product[x * cells : (x + 1) * cells]

    for o in range(1, XCHIPS):
        slice_copy(o).start()
        code_copy(o).start()
    total[...] = jnp.zeros_like(total)
    partial[...] = jnp.zeros_like(partial)

    def tick(s, carry):
        @pl.when(s == 1)
        def _():
            for o in range(1, XCHIPS):
                slice_copy(o).wait_recv()
            for o in range(1, 8):
                z_copy(o).start()

        @pl.when(s == Y_TICK)
        def _():
            for o in range(1, 8):
                z_copy(o).wait_recv()
            for o in range(1, 4):
                y_copy(o).start()

        @pl.when(s == CORE_TICK)
        def _():
            for o in range(1, 4):
                y_copy(o).wait_recv()
            core_copy().start()
            for o in range(1, XCHIPS):
                code_copy(o).wait_recv()
            codes_copy().start()

        for k in reversed(range(steps)):
            g = s - offsets[k]

            @pl.when((g >= 0) & (g < groups))
            def _():
                send(g, k)

        @pl.when(s < groups - 2)
        def _():
            own_blocks(s + 1)

        @pl.when(s == groups - 2)
        def _():
            last_blocks()

        @pl.when((s >= ARRANGE_TICK) & (s < ARRANGE_TICK + slots * ROWS // 128))
        def _():
            arrange(s - ARRANGE_TICK)

        @pl.when(s == COARSE_TICK)
        def _():
            core_copy().wait_recv()
            codes_copy().wait()

        @pl.when((s >= COARSE_TICK) & (s < COARSE_TICK + slots // CHUNK))
        def _():
            coarse_chunk(s - COARSE_TICK)

        @pl.when(s == COARSE_TICK + slots // CHUNK - 1)
        def _():
            for o in range(1, XCHIPS):
                sum_copy(o).start()

        g = s - offsets[steps]

        @pl.when((g >= 0) & (g < groups))
        def _():
            multiply(g)

        return carry

    lax.fori_loop(0, groups + offsets[steps], tick, 0)

    def drain(g, carry):
        for k in range(steps):
            copy(g, k).wait_send()
        return carry

    lax.fori_loop(0, groups, drain, 0)

    for o in range(1, XCHIPS):
        sum_copy(o).wait_recv()
    coarse_out_ref[...] = (
        (partial[chip] + incoming[x_peer(1)]) + (incoming[x_peer(2)] + incoming[x_peer(3)])
    )[:, :coef]
    for o in range(1, XCHIPS):
        slice_copy(o).wait_send()
        code_copy(o).wait_send()
        sum_copy(o).wait_send()
        y_copy(o).wait_send()
    for o in range(1, 8):
        z_copy(o).wait_send()
    core_copy().wait_send()

    live = live_ref[0]
    side = lanes_below((coef, 128), 64)

    def finish(p, carry):
        left = total[:coef, pl.ds(pl.multiple_of(p * 256, 256), 128)]
        right = total[:coef, pl.ds(pl.multiple_of(p * 256 + 128, 128), 128)]
        left = left + pltpu.roll(left, 64, 1)
        right = right + pltpu.roll(right, 64, 1)
        both = jnp.where(side, left, right)
        position = 2 * p + jnp.where(side, 0, 1)
        out_ref[:, pl.ds(pl.multiple_of(p * 128, 128), 128)] = jnp.where(position < live, both, 0.0)
        return carry

    lax.fori_loop(0, own // 2, finish, 0)


def source_codes(coarse_lists):
    cells, slots = coarse_lists.shape
    index = jnp.maximum(coarse_lists, 0)
    cell, device = index % cells, index // cells
    gy, gx = device % 32, device // 32
    place = (((gx % 2) * 4 + gy % 4) * 8 + gy // 4) * XCHIPS + gx // 2
    code = (place * PACKED + cell % PACKED) * 4 + cell // PACKED
    code = jnp.where(coarse_lists < 0, 3, code).astype(jnp.int32)
    by_slot = jnp.pad(code.T, ((0, 0), (0, 128 - cells)))
    by_cell = jnp.pad(code, ((0, 0), (0, 128 - slots)))
    return jnp.concatenate([by_slot, by_cell], axis=0)


def shards(multipoles, coarse_poles, operators, block_lists, coarse_lists, send_lists, live_blocks):
    coef, cells = multipoles.shape
    slots = operators.shape[0]
    coarse_cells = coarse_poles.shape[1]
    own = cells // BCELLS
    _, steps, sent = send_lists.shape
    groups = -(-coef // ROWS)
    height = groups * ROWS
    held = own + steps * sent
    low_bits = lax.axis_size("gy").bit_length() - 1
    offsets = (0, 1, 2, 4, 6, 8, 9, 10, 11)
    vmem = pl.BlockSpec(memory_space=pltpu.VMEM)
    smem = pl.BlockSpec(memory_space=pltpu.SMEM)
    f32, bf16, dma = jnp.float32, jnp.bfloat16, pltpu.SemaphoreType.DMA
    fine_local, coarse_local = pl.pallas_call(
        functools.partial(fine_kernel, groups, steps, own, sent, low_bits, offsets),
        out_shape=(
            jax.ShapeDtypeStruct((coef, cells), f32),
            jax.ShapeDtypeStruct((coarse_cells, coef), f32),
        ),
        in_specs=[vmem, vmem, pl.BlockSpec(memory_space=pl.ANY), vmem, smem, smem, smem],
        out_specs=(vmem, vmem),
        scratch_shapes=[
            pltpu.VMEM((groups, held, 8, 128), f32),
            pltpu.VMEM((groups, steps, sent, 8, 128), f32),
            pltpu.VMEM((groups, steps, sent, 8, 128), f32),
            pltpu.VMEM((held + 1, ROWS, 128), bf16),
            pltpu.VMEM((groups, 2 * height, slots * ROWS), bf16),
            pltpu.VMEM((height, own * 128), f32),
            pltpu.VMEM((slots, coef, coef), f32),
            pltpu.VMEM((XCHIPS, PACKED, 128), f32),
            pltpu.VMEM((64 * XCHIPS * PACKED, 128), f32),
            pltpu.VMEM((XCHIPS, slots + coarse_cells, 128), jnp.int32),
            pltpu.SMEM((XCHIPS, slots, 128), jnp.int32),
            pltpu.VMEM((2 * height, slots * 128), bf16),
            pltpu.VMEM((CHUNK, XCHIPS * coarse_cells, 128), f32),
            pltpu.VMEM((XCHIPS, coarse_cells, height), f32),
            pltpu.VMEM((XCHIPS, coarse_cells, height), f32),
            dma((groups, steps)),
            dma((groups, steps)),
            dma((slots,)),
            dma((XCHIPS - 1,)),
            dma((XCHIPS - 1,)),
            dma((XCHIPS - 1,)),
            dma((XCHIPS - 1,)),
            dma((7,)),
            dma((7,)),
            dma((3,)),
            dma((3,)),
            dma,
            dma,
            dma((XCHIPS - 1,)),
            dma((XCHIPS - 1,)),
            dma,
        ],
        compiler_params=pltpu.CompilerParams(
            collective_id=0, has_side_effects=True, vmem_limit_bytes=62 << 20
        ),
        cost_estimate=pl.CostEstimate(
            flops=8 * slots * coef * coef * cells, bytes_accessed=8 << 20, transcendentals=0
        ),
        name="far_field",
    )(
        multipoles,
        coarse_poles.T,
        operators.transpose(1, 0, 2),
        source_codes(coarse_lists),
        send_lists[0],
        block_lists,
        live_blocks,
    )
    return (fine_local, coarse_local.T)


def solution(mesh):
    return jax.shard_map(
        shards,
        mesh=mesh,
        in_specs=(
            P(None, ("gx", "gy")),
            P(None, ("gx", "gy")),
            P(),
            P(("gx", "gy"), None),
            P(("gx", "gy"), None),
            P(("gx", "gy"), None, None),
            P(("gx", "gy")),
        ),
        out_specs=(P(None, ("gx", "gy")), P(None, ("gx", "gy"))),
        check_vma=False,
    )
```

```python
import functools
import jax
import jax.numpy as jnp
from jax import lax
from jax.experimental import pallas as pl
from jax.experimental.pallas import tpu as pltpu
from jax.sharding import PartitionSpec as P

BCELLS = 64
ROWS = 16
XCHIPS = 4
WIDTH = 42
PARTS = 3
PACKED = 24
CHUNK = 4
WIDE = 16
STRIDE = 2
OFFSETS = (0, 2, 4, 6, 9, 13, 15, 17, 19)
X_TICK, Y_TICK, CORE_TICK, COARSE_TICK = 2, 5, 12, 20
ARRANGE_TICK, ARRANGE_STEP = 4, 4
MESH = pl.DeviceIdType.MESH


def lanes_below(shape, limit):
    return lax.broadcasted_iota(jnp.int32, shape, len(shape) - 1) < limit


def fine_kernel(
    groups, steps, own, sent, low_bits, offsets,
    mult_ref, coarse_ref, ops_hbm, codes_ref, send_ref, lists_ref, live_ref,
    out_ref, coarse_out_ref,
    table, outgo, landed, split, mats, total, ops_ref,
    packed, everything, codes, codes_smem, replicas, gathered, partial, incoming,
    send_sem, recv_sem, ops_sem, slice_send, slice_recv, code_send, code_recv,
    z_send, z_recv, y_send, y_recv, core_send, core_recv, sum_send, sum_recv, smem_sem,
):
    slots, coef, _ = ops_ref.shape
    gx = lax.axis_index("gx")
    gy = lax.axis_index("gy")
    chip, core = gx // 2, lax.rem(gx, 2)
    z, y = gy // 4, lax.rem(gy, 4)
    cells = coarse_ref.shape[0]

    def x_peer(o):
        return lax.rem(chip + o, XCHIPS)

    def x_device(o):
        return (x_peer(o) * 2 + core, gy)

    def z_device(o):
        return (gx, lax.rem(z + o, 8) * 4 + y)

    def y_device(o):
        return (gx, z * 4 + lax.rem(y + o, 4))

    def core_device():
        return (gx + 1 - 2 * core, gy)

    def rows_of(c, yy, zz, xx, count):
        at = (((c * 4 + yy) * 8 + zz) * XCHIPS + xx) * PACKED
        return pl.ds(pl.multiple_of(at, 8), count * PACKED)

    def remote(source, target, send, recv, device):
        return pltpu.make_async_remote_copy(
            src_ref=source, dst_ref=target, send_sem=send, recv_sem=recv,
            device_id=device, device_id_type=MESH,
        )

    def slice_copy(o):
        return remote(
            packed.at[x_peer(o)], everything.at[rows_of(core, y, z, chip, 1)],
            slice_send.at[o - 1], slice_recv.at[o - 1], x_device(o),
        )

    def code_copy(o):
        return remote(
            codes_ref, codes.at[chip], code_send.at[o - 1], code_recv.at[o - 1], x_device(o)
        )

    def z_copy(o):
        rows = rows_of(core, y, z, 0, XCHIPS)
        return remote(
            everything.at[rows], everything.at[rows], z_send.at[o - 1], z_recv.at[o - 1], z_device(o)
        )

    def y_copy(o):
        rows = rows_of(core, y, 0, 0, 8 * XCHIPS)
        return remote(
            everything.at[rows], everything.at[rows], y_send.at[o - 1], y_recv.at[o - 1], y_device(o)
        )

    def core_copy():
        rows = rows_of(core, 0, 0, 0, 32 * XCHIPS)
        return remote(everything.at[rows], everything.at[rows], core_send, core_recv, core_device())

    def sum_copy(o):
        return remote(
            partial.at[x_peer(o)], incoming.at[chip],
            sum_send.at[o - 1], sum_recv.at[o - 1], x_device(o),
        )

    def ops_copy(j):
        return pltpu.make_async_copy(ops_hbm.at[:, j, :], ops_ref.at[j], ops_sem.at[j])

    def codes_copy():
        return pltpu.make_async_copy(codes.at[:, 0:slots], codes_smem, smem_sem)

    def partner(k):
        if k < low_bits:
            bit = 1 << k
            up = lax.rem(gy // bit, 2)
            return (gx, gy + bit - 2 * bit * up)
        bit = 1 << (k - low_bits)
        up = lax.rem(gx // bit, 2)
        return (gx + bit - 2 * bit * up, gy)

    def copy(g, k):
        return pltpu.make_async_remote_copy(
            src_ref=outgo.at[g, k],
            dst_ref=landed.at[g, k],
            send_sem=send_sem.at[g, k],
            recv_sem=recv_sem.at[g, k],
            device_id=partner(k),
            device_id_type=MESH,
        )

    barrier = pltpu.get_barrier_semaphore()
    peers = [x_device(o) for o in range(1, XCHIPS)] + [z_device(o) for o in range(1, 8)]
    peers += [y_device(o) for o in range(1, 4)] + [core_device()]
    for peer in peers:
        pl.semaphore_signal(barrier, inc=1, device_id=peer, device_id_type=MESH)
    lax.fori_loop(0, slots, lambda j, c: (ops_copy(j).start(), c)[1], 0)

    lane64 = lax.broadcasted_iota(jnp.int32, (cells, 128), 1)
    near = coarse_ref[:, :128]
    far = jnp.concatenate(
        [coarse_ref[:, 128:], jnp.zeros((cells, 256 - coef), jnp.float32)], axis=1
    )
    for x in range(XCHIPS):
        shift = (128 - WIDTH * x) % 128
        base = pltpu.roll(near, shift, 1) if shift else near
        if x == XCHIPS - 1:
            base = jnp.where(lane64 < shift, base, pltpu.roll(far, shift, 1))
        base = jnp.where(lane64 < WIDTH, base, 0.0)
        rest = jnp.concatenate(
            [base[2 * PACKED :], jnp.zeros((3 * PACKED - cells, 128), jnp.float32)], axis=0
        )
        packed[x] = (
            base[:PACKED]
            + pltpu.roll(base[PACKED : 2 * PACKED], WIDTH, 1)
            + pltpu.roll(rest, 2 * WIDTH, 1)
        )
    everything[rows_of(core, y, z, chip, 1)] = packed[chip]
    codes[chip] = codes_ref[...]

    half = lanes_below((8, 128), 64)

    def place(g, p, first, second):
        table[g, 2 * p] = jnp.where(half, first, pltpu.roll(second, 64, 1))
        table[g, 2 * p + 1] = jnp.where(half, pltpu.roll(first, 64, 1), second)

    def own_blocks(g):
        def pair(p, c):
            lanes = pl.ds(pl.multiple_of(p * 128, 128), 128)
            first = mult_ref[pl.ds(pl.multiple_of(g * ROWS, 8), 8), lanes]
            second = mult_ref[pl.ds(pl.multiple_of(g * ROWS + 8, 8), 8), lanes]
            place(g, p, first, second)
            return c

        lax.fori_loop(0, own // 2, pair, 0, unroll=True)

    def last_blocks():
        g = groups - 1
        left = coef - g * ROWS

        def pair(p, c):
            lanes = pl.ds(pl.multiple_of(p * 128, 128), 128)
            first = jnp.concatenate(
                [mult_ref[g * ROWS : coef, lanes], jnp.zeros((8 - left, 128), jnp.float32)], axis=0
            )
            place(g, p, first, jnp.zeros((8, 128), jnp.float32))
            return c

        lax.fori_loop(0, own // 2, pair, 0)

    own_blocks(0)
    split[0] = jnp.zeros((ROWS, 128), jnp.bfloat16)
    pl.semaphore_wait(barrier, len(peers))

    def send(g, k):
        if k > 0:
            copy(g, k - 1).wait_recv()
            first = own + (k - 1) * sent
            table[g, first : first + sent] = landed[g, k - 1]
        for i in range(sent):
            outgo[g, k, i] = table[g, send_ref[k, i]]
        copy(g, k).start()

    def arrange(n):
        q, at = n // groups, pl.multiple_of(lax.rem(n, groups) * ROWS, ROWS)
        per = 128 // ROWS
        lane = lax.broadcasted_iota(jnp.int32, (ROWS, 128), 1)
        tail = coef - 128
        beyond = (lane >= 2) & (jnp.full((ROWS, 128), chip, jnp.int32) == XCHIPS - 1)

        def rows_at(read, at):
            tiles = []
            for i in range(per):
                full = read(q * per + i)
                tiles.append(
                    (
                        full[:, :128],
                        jnp.concatenate(
                            [full[:, 128:], jnp.zeros((ROWS, 128 - tail), jnp.float32)], axis=1
                        ),
                    )
                )
            height = mats.shape[1] // 2
            for i in range(per):
                base = pltpu.roll(tiles[i][0], lax.rem(128 - WIDTH * chip, 128), 1)
                base = jnp.where(beyond, pltpu.roll(tiles[i][1], 2, 1), base)
                base = jnp.where(lane < WIDTH, base, 0.0)
                base = base + pltpu.roll(base, WIDTH, 1) + pltpu.roll(base, 2 * WIDTH, 1)
                high = base.astype(jnp.bfloat16)
                low = (base - high.astype(jnp.float32)).astype(jnp.bfloat16)
                lanes = pl.ds(pl.multiple_of((q * per + i) * 128, 128), 128)
                replicas[pl.ds(at, ROWS), lanes] = high
                replicas[pl.ds(height + at, ROWS), lanes] = low
            for g in range(groups):
                which, at_lane = divmod(g * ROWS, 128)
                value = jnp.zeros((ROWS, 128), jnp.float32)
                for i in range(per):
                    shift = (i * ROWS - at_lane) % 128
                    piece = tiles[i][which]
                    if shift:
                        piece = pltpu.roll(piece, shift, 1)
                    value = jnp.where((lane >= i * ROWS) & (lane < (i + 1) * ROWS), piece, value)
                high = value.astype(jnp.bfloat16)
                low = (value - high.astype(jnp.float32)).astype(jnp.bfloat16)
                mats[g, pl.ds(at, ROWS), pl.ds(pl.multiple_of(q * 128, 128), 128)] = high
                mats[g, pl.ds(height + at, ROWS), pl.ds(pl.multiple_of(q * 128, 128), 128)] = low

        whole = coef // ROWS
        left = coef - whole * ROWS

        @pl.when(lax.rem(n, groups) < whole)
        def _():
            rows_at(lambda j: ops_ref[j, pl.ds(at, ROWS), :], at)

        @pl.when(lax.rem(n, groups) == whole)
        def _():
            rows_at(
                lambda j: jnp.concatenate(
                    [
                        ops_ref[j, whole * ROWS : coef, :],
                        jnp.zeros((ROWS - left, coef), jnp.float32),
                    ],
                    axis=0,
                ),
                whole * ROWS,
            )

    def multiply(g):
        copy(g, steps - 1).wait_recv()
        first = own + (steps - 1) * sent
        table[g, first : first + sent] = landed[g, steps - 1]
        halves = lanes_below((16, 8, 128), 64)

        def cut(c, carry):
            at = pl.multiple_of(c * 16, 16)
            block = table[g, pl.ds(at, 16)]
            high = block.astype(jnp.bfloat16).astype(jnp.float32)
            low = block - high
            top = jnp.where(halves, high, pltpu.roll(low, 64, 2))
            bottom = jnp.where(halves, pltpu.roll(high, 64, 2), low)
            split[pl.ds(at + 1, 16)] = jnp.concatenate([top, bottom], axis=1).astype(jnp.bfloat16)
            return carry

        lax.fori_loop(0, (own + steps * sent) // 16, cut, 0, unroll=True)
        height = mats.shape[1] // 2

        def targets(p, carry):
            sides = []
            for side in range(WIDE):
                sides.append(
                    jnp.concatenate(
                        [split[lists_ref[WIDE * p + side, j] + 1] for j in range(slots)], axis=0
                    )
                )
            source = jnp.concatenate(sides, axis=1)
            product = jnp.dot(mats[g], source, preferred_element_type=jnp.float32)
            lanes = pl.ds(pl.multiple_of(p * WIDE * 128, WIDE * 128), WIDE * 128)
            total[:, lanes] += product[:height] + product[height:]
            return carry

        lax.fori_loop(0, own // WIDE, targets, 0)

    lane = lax.broadcasted_iota(jnp.int32, (cells, 128), 1)
    part_of = jnp.where(lane < WIDTH, 0, jnp.where(lane < 2 * WIDTH, 1, jnp.where(lane < 3 * WIDTH, 2, 7)))

    def coarse_chunk(c):
        for i in range(CHUNK):
            def take(x, carry, i=i):
                for r in range(cells):
                    row = codes_smem[x, c * CHUNK + i, r]
                    gathered[i, pl.ds(pl.multiple_of(x * cells, 8) + r, 1), :] = everything[
                        pl.ds(row, 1), :
                    ]
                return carry

            lax.fori_loop(0, XCHIPS, take, 0)
        highs, lows = [], []
        for x in range(XCHIPS):
            turned = pltpu.roll(codes[x, slots : slots + cells, :], lax.rem(128 - c * CHUNK, 128), 1)
            row_high, row_low = [], []
            for i in range(CHUNK):
                value = gathered[i, x * cells : (x + 1) * cells]
                value = jnp.where(part_of == turned[:, i : i + 1], value, 0.0)
                high = value.astype(jnp.bfloat16)
                row_high.append(high)
                row_low.append((value - high.astype(jnp.float32)).astype(jnp.bfloat16))
            highs.append(jnp.concatenate(row_high, axis=1))
            lows.append(jnp.concatenate(row_low, axis=1))
        high = jnp.concatenate(highs, axis=0)
        low = jnp.concatenate(lows, axis=0)
        height = mats.shape[1] // 2
        lanes = pl.ds(pl.multiple_of(c * CHUNK * 128, CHUNK * 128), CHUNK * 128)
        op_high = replicas[:height, lanes]
        op_low = replicas[height:, lanes]
        dims = (((1,), (1,)), ((), ()))

        def dot(a, b):
            return lax.dot_general(a, b, dims, preferred_element_type=jnp.float32)

        product = dot(high, op_high) + dot(low, op_high) + dot(high, op_low)
        for x in range(XCHIPS):
            partial[x] += product[x * cells : (x + 1) * cells]

    for o in range(1, XCHIPS):
        slice_copy(o).start()
        code_copy(o).start()
    total[...] = jnp.zeros_like(total)
    partial[...] = jnp.zeros_like(partial)

    def tick(s, carry):
        @pl.when(s == X_TICK)
        def _():
            for o in range(1, XCHIPS):
                slice_copy(o).wait_recv()
            for o in range(1, 8):
                z_copy(o).start()

        @pl.when(s == Y_TICK)
        def _():
            for o in range(1, 8):
                z_copy(o).wait_recv()
            for o in range(1, 4):
                y_copy(o).start()

        @pl.when(s == CORE_TICK)
        def _():
            for o in range(1, 4):
                y_copy(o).wait_recv()
            core_copy().start()
            for o in range(1, XCHIPS):
                code_copy(o).wait_recv()
            codes_copy().start()

        for k in reversed(range(steps)):
            late = s - offsets[k]
            g = late // STRIDE

            @pl.when((late >= 0) & (g < groups) & (lax.rem(late, STRIDE) == 0))
            def _():
                send(g, k)

        g = s // STRIDE + 1

        @pl.when((g < groups - 1) & (lax.rem(s, STRIDE) == 0))
        def _():
            own_blocks(g)

        @pl.when((g == groups - 1) & (lax.rem(s, STRIDE) == 0))
        def _():
            last_blocks()

        @pl.when(s == ARRANGE_TICK)
        def _():
            lax.fori_loop(0, slots, lambda j, c: (ops_copy(j).wait(), c)[1], 0)

        first = (s - ARRANGE_TICK) * ARRANGE_STEP
        last = jnp.minimum(first + ARRANGE_STEP, groups * slots * ROWS // 128)

        @pl.when(first >= 0)
        def _():
            lax.fori_loop(first, last, lambda n, c: (arrange(n), c)[1], 0)

        @pl.when(s == COARSE_TICK)
        def _():
            core_copy().wait_recv()
            codes_copy().wait()

        @pl.when((s >= COARSE_TICK) & (s < COARSE_TICK + slots // CHUNK))
        def _():
            coarse_chunk(s - COARSE_TICK)

        @pl.when(s == COARSE_TICK + slots // CHUNK - 1)
        def _():
            for o in range(1, XCHIPS):
                sum_copy(o).start()

        late = s - offsets[steps]
        g = late // STRIDE

        @pl.when((late >= 0) & (g < groups) & (lax.rem(late, STRIDE) == 0))
        def _():
            multiply(g)

        return carry

    lax.fori_loop(0, (groups - 1) * STRIDE + offsets[steps] + 1, tick, 0)

    def drain(g, carry):
        for k in range(steps):
            copy(g, k).wait_send()
        return carry

    lax.fori_loop(0, groups, drain, 0)

    for o in range(1, XCHIPS):
        sum_copy(o).wait_recv()
    coarse_out_ref[...] = (
        (partial[chip] + incoming[x_peer(1)]) + (incoming[x_peer(2)] + incoming[x_peer(3)])
    )[:, :coef]
    for o in range(1, XCHIPS):
        slice_copy(o).wait_send()
        code_copy(o).wait_send()
        sum_copy(o).wait_send()
        y_copy(o).wait_send()
    for o in range(1, 8):
        z_copy(o).wait_send()
    core_copy().wait_send()

    live = live_ref[0]
    side = lanes_below((coef, 128), 64)

    def finish(p, carry):
        left = total[:coef, pl.ds(pl.multiple_of(p * 256, 256), 128)]
        right = total[:coef, pl.ds(pl.multiple_of(p * 256 + 128, 128), 128)]
        left = left + pltpu.roll(left, 64, 1)
        right = right + pltpu.roll(right, 64, 1)
        both = jnp.where(side, left, right)
        position = 2 * p + jnp.where(side, 0, 1)
        out_ref[:, pl.ds(pl.multiple_of(p * 128, 128), 128)] = jnp.where(position < live, both, 0.0)
        return carry

    lax.fori_loop(0, own // 2, finish, 0)


def source_codes(coarse_lists):
    cells, slots = coarse_lists.shape
    index = jnp.maximum(coarse_lists, 0)
    cell, device = index % cells, index // cells
    gy, gx = device % 32, device // 32
    place = (((gx % 2) * 4 + gy % 4) * 8 + gy // 4) * XCHIPS + gx // 2
    row = (place * PACKED + cell % PACKED).astype(jnp.int32)
    part = jnp.where(coarse_lists < 0, PARTS, cell // PACKED).astype(jnp.int32)
    by_slot = jnp.pad(row.T, ((0, 0), (0, 128 - cells)))
    by_cell = jnp.pad(part, ((0, 0), (0, 128 - slots)))
    return jnp.concatenate([by_slot, by_cell], axis=0)


def shards(multipoles, coarse_poles, operators, block_lists, coarse_lists, send_lists, live_blocks):
    coef, cells = multipoles.shape
    slots = operators.shape[0]
    coarse_cells = coarse_poles.shape[1]
    own = cells // BCELLS
    _, steps, sent = send_lists.shape
    groups = -(-coef // ROWS)
    height = groups * ROWS
    held = own + steps * sent
    low_bits = lax.axis_size("gy").bit_length() - 1
    offsets = OFFSETS
    vmem = pl.BlockSpec(memory_space=pltpu.VMEM)
    smem = pl.BlockSpec(memory_space=pltpu.SMEM)
    f32, bf16, dma = jnp.float32, jnp.bfloat16, pltpu.SemaphoreType.DMA
    fine_local, coarse_local = pl.pallas_call(
        functools.partial(fine_kernel, groups, steps, own, sent, low_bits, offsets),
        out_shape=(
            jax.ShapeDtypeStruct((coef, cells), f32),
            jax.ShapeDtypeStruct((coarse_cells, coef), f32),
        ),
        in_specs=[vmem, vmem, pl.BlockSpec(memory_space=pl.ANY), vmem, smem, smem, smem],
        out_specs=(vmem, vmem),
        scratch_shapes=[
            pltpu.VMEM((groups, held, 8, 128), f32),
            pltpu.VMEM((groups, steps, sent, 8, 128), f32),
            pltpu.VMEM((groups, steps, sent, 8, 128), f32),
            pltpu.VMEM((held + 1, ROWS, 128), bf16),
            pltpu.VMEM((groups, 2 * height, slots * ROWS), bf16),
            pltpu.VMEM((height, own * 128), f32),
            pltpu.VMEM((slots, coef, coef), f32),
            pltpu.VMEM((XCHIPS, PACKED, 128), f32),
            pltpu.VMEM((64 * XCHIPS * PACKED, 128), f32),
            pltpu.VMEM((XCHIPS, slots + coarse_cells, 128), jnp.int32),
            pltpu.SMEM((XCHIPS, slots, 128), jnp.int32),
            pltpu.VMEM((2 * height, slots * 128), bf16),
            pltpu.VMEM((CHUNK, XCHIPS * coarse_cells, 128), f32),
            pltpu.VMEM((XCHIPS, coarse_cells, height), f32),
            pltpu.VMEM((XCHIPS, coarse_cells, height), f32),
            dma((groups, steps)),
            dma((groups, steps)),
            dma((slots,)),
            dma((XCHIPS - 1,)),
            dma((XCHIPS - 1,)),
            dma((XCHIPS - 1,)),
            dma((XCHIPS - 1,)),
            dma((7,)),
            dma((7,)),
            dma((3,)),
            dma((3,)),
            dma,
            dma,
            dma((XCHIPS - 1,)),
            dma((XCHIPS - 1,)),
            dma,
        ],
        compiler_params=pltpu.CompilerParams(
            collective_id=0, has_side_effects=True, vmem_limit_bytes=62 << 20
        ),
        cost_estimate=pl.CostEstimate(
            flops=8 * slots * coef * coef * cells, bytes_accessed=8 << 20, transcendentals=0
        ),
        name="far_field",
    )(
        multipoles,
        coarse_poles.T,
        operators.transpose(1, 0, 2),
        source_codes(coarse_lists),
        send_lists[0],
        block_lists,
        live_blocks,
    )
    return (fine_local, coarse_local.T)


def solution(mesh):
    return jax.shard_map(
        shards,
        mesh=mesh,
        in_specs=(
            P(None, ("gx", "gy")),
            P(None, ("gx", "gy")),
            P(),
            P(("gx", "gy"), None),
            P(("gx", "gy"), None),
            P(("gx", "gy"), None, None),
            P(("gx", "gy")),
        ),
        out_specs=(P(None, ("gx", "gy")), P(None, ("gx", "gy"))),
        check_vma=False,
    )
```

```python
import functools
import jax
import jax.numpy as jnp
from jax import lax
from jax.experimental import pallas as pl
from jax.experimental.pallas import tpu as pltpu
from jax.sharding import PartitionSpec as P

BCELLS = 64
ROWS = 16
XCHIPS = 4
WIDTH = 42
PARTS = 3
PACKED = 24
CHUNK = 4
WIDE = 16
STRIDES = (1, 1, 1, 1, 1, 1, 1, 1, 1)
ORDER = (0, 1, 2, 3, 4, 5, 6, 7)
OFFSETS = (0, 1, 2, 3, 4, 6, 7, 8, 9)
X_TICK, Y_TICK, CORE_TICK, COARSE_TICK = 1, 5, 9, 11
ARRANGE_TICK, ARRANGE_STEP = 2, 6
MESH = pl.DeviceIdType.MESH


def lanes_below(shape, limit):
    return lax.broadcasted_iota(jnp.int32, shape, len(shape) - 1) < limit


def fine_kernel(
    groups, steps, own, sent, low_bits, offsets,
    mult_ref, coarse_ref, ops_hbm, codes_ref, send_ref, lists_ref,
    out_ref, coarse_out_ref,
    table, outgo, landed, split, mats, total, ops_ref,
    packed, everything, codes, codes_smem, replicas, gathered, partial, incoming,
    send_sem, recv_sem, ops_sem, slice_send, slice_recv, code_send, code_recv,
    z_send, z_recv, y_send, y_recv, core_send, core_recv, sum_send, sum_recv, smem_sem,
):
    slots, coef, _ = ops_ref.shape
    gx = lax.axis_index("gx")
    gy = lax.axis_index("gy")
    chip, core = gx // 2, lax.rem(gx, 2)
    z, y = gy // 4, lax.rem(gy, 4)
    cells = coarse_ref.shape[0]

    def x_peer(o):
        return lax.rem(chip + o, XCHIPS)

    def x_device(o):
        return (x_peer(o) * 2 + core, gy)

    def z_device(o):
        return (gx, lax.rem(z + o, 8) * 4 + y)

    def y_device(o):
        return (gx, z * 4 + lax.rem(y + o, 4))

    def core_device():
        return (gx + 1 - 2 * core, gy)

    def rows_of(c, yy, zz, xx, count):
        at = (((c * 4 + yy) * 8 + zz) * XCHIPS + xx) * PACKED
        return pl.ds(pl.multiple_of(at, 8), count * PACKED)

    def remote(source, target, send, recv, device):
        return pltpu.make_async_remote_copy(
            src_ref=source, dst_ref=target, send_sem=send, recv_sem=recv,
            device_id=device, device_id_type=MESH,
        )

    def slice_copy(o):
        return remote(
            packed.at[x_peer(o)], everything.at[rows_of(core, y, z, chip, 1)],
            slice_send.at[o - 1], slice_recv.at[o - 1], x_device(o),
        )

    def code_copy(o):
        return remote(
            codes_ref, codes.at[chip], code_send.at[o - 1], code_recv.at[o - 1], x_device(o)
        )

    def z_copy(o):
        rows = rows_of(core, y, z, 0, XCHIPS)
        return remote(
            everything.at[rows], everything.at[rows], z_send.at[o - 1], z_recv.at[o - 1], z_device(o)
        )

    def y_copy(o):
        rows = rows_of(core, y, 0, 0, 8 * XCHIPS)
        return remote(
            everything.at[rows], everything.at[rows], y_send.at[o - 1], y_recv.at[o - 1], y_device(o)
        )

    def core_copy():
        rows = rows_of(core, 0, 0, 0, 32 * XCHIPS)
        return remote(everything.at[rows], everything.at[rows], core_send, core_recv, core_device())

    def sum_copy(o):
        return remote(
            partial.at[x_peer(o)], incoming.at[chip],
            sum_send.at[o - 1], sum_recv.at[o - 1], x_device(o),
        )

    def ops_copy(j):
        return pltpu.make_async_copy(ops_hbm.at[:, j, :], ops_ref.at[j], ops_sem.at[j])

    def codes_copy():
        return pltpu.make_async_copy(codes.at[:, 0:slots], codes_smem, smem_sem)

    def partner(k):
        if k < low_bits:
            bit = 1 << k
            up = lax.rem(gy // bit, 2)
            return (gx, gy + bit - 2 * bit * up)
        bit = 1 << (k - low_bits)
        up = lax.rem(gx // bit, 2)
        return (gx + bit - 2 * bit * up, gy)

    def copy(g, k, count=sent):
        return pltpu.make_async_remote_copy(
            src_ref=outgo.at[g, k, pl.ds(0, count)],
            dst_ref=landed.at[g, k, pl.ds(0, count)],
            send_sem=send_sem.at[g, k],
            recv_sem=recv_sem.at[g, k],
            device_id=partner(k),
            device_id_type=MESH,
        )

    def receive(g, k):
        first = own + k * sent

        @pl.when(g < groups - 1)
        def _():
            copy(g, k).wait_recv()
            table[g, first : first + sent] = landed[g, k]

        @pl.when(g == groups - 1)
        def _():
            copy(g, k, sent // 2).wait_recv()
            for i in range(sent // 2):
                both = landed[g, k, i]
                table[g, first + i] = jnp.where(half, both, 0.0)
                table[g, first + sent // 2 + i] = jnp.where(half, pltpu.roll(both, 64, 1), 0.0)

    barrier = pltpu.get_barrier_semaphore()
    peers = [x_device(o) for o in range(1, XCHIPS)] + [z_device(o) for o in range(1, 8)]
    peers += [y_device(o) for o in range(1, 4)] + [core_device()]
    for peer in peers:
        pl.semaphore_signal(barrier, inc=1, device_id=peer, device_id_type=MESH)

    lane64 = lax.broadcasted_iota(jnp.int32, (cells, 128), 1)
    near = coarse_ref[:, :128]
    far = jnp.concatenate(
        [coarse_ref[:, 128:], jnp.zeros((cells, 256 - coef), jnp.float32)], axis=1
    )
    for x in range(XCHIPS):
        shift = (128 - WIDTH * x) % 128
        base = pltpu.roll(near, shift, 1) if shift else near
        if x == XCHIPS - 1:
            base = jnp.where(lane64 < shift, base, pltpu.roll(far, shift, 1))
        base = jnp.where(lane64 < WIDTH, base, 0.0)
        rest = jnp.concatenate(
            [base[2 * PACKED :], jnp.zeros((3 * PACKED - cells, 128), jnp.float32)], axis=0
        )
        packed[x] = (
            base[:PACKED]
            + pltpu.roll(base[PACKED : 2 * PACKED], WIDTH, 1)
            + pltpu.roll(rest, 2 * WIDTH, 1)
        )
    everything[rows_of(core, y, z, chip, 1)] = packed[chip]
    codes[chip] = codes_ref[...]

    half = lanes_below((8, 128), 64)

    def place(g, p, first, second):
        table[g, 2 * p] = jnp.where(half, first, pltpu.roll(second, 64, 1))
        table[g, 2 * p + 1] = jnp.where(half, pltpu.roll(first, 64, 1), second)

    def own_blocks(g):
        def pair(p, c):
            lanes = pl.ds(pl.multiple_of(p * 128, 128), 128)
            first = mult_ref[pl.ds(pl.multiple_of(g * ROWS, 8), 8), lanes]
            second = mult_ref[pl.ds(pl.multiple_of(g * ROWS + 8, 8), 8), lanes]
            place(g, p, first, second)
            return c

        lax.fori_loop(0, own // 2, pair, 0, unroll=True)

    def last_blocks():
        g = groups - 1
        left = coef - g * ROWS

        def pair(p, c):
            lanes = pl.ds(pl.multiple_of(p * 128, 128), 128)
            first = jnp.concatenate(
                [mult_ref[g * ROWS : coef, lanes], jnp.zeros((8 - left, 128), jnp.float32)], axis=0
            )
            place(g, p, first, jnp.zeros((8, 128), jnp.float32))
            return c

        lax.fori_loop(0, own // 2, pair, 0)

    split[0] = jnp.zeros((ROWS, 128), jnp.bfloat16)
    pl.semaphore_wait(barrier, len(peers))

    def send(g, k):
        if k == 0:

            @pl.when(g < groups - 1)
            def _():
                own_blocks(g)

            @pl.when(g == groups - 1)
            def _():
                last_blocks()

        if k > 0:
            receive(g, k - 1)

        @pl.when(g < groups - 1)
        def _():
            for i in range(sent):
                outgo[g, k, i] = table[g, send_ref[k, i]]
            copy(g, k).start()

        @pl.when(g == groups - 1)
        def _():
            for i in range(sent // 2):
                other = pltpu.roll(table[g, send_ref[k, sent // 2 + i]], 64, 1)
                outgo[g, k, i] = jnp.where(half, table[g, send_ref[k, i]], other)
            copy(g, k, sent // 2).start()

    def arrange(n):
        q, at = n // groups, pl.multiple_of(lax.rem(n, groups) * ROWS, ROWS)
        per = 128 // ROWS
        lane = lax.broadcasted_iota(jnp.int32, (ROWS, 128), 1)
        tail = coef - 128
        beyond = (lane >= 2) & (jnp.full((ROWS, 128), chip, jnp.int32) == XCHIPS - 1)

        def rows_at(read, at):
            tiles = []
            for i in range(per):
                full = read(q * per + i)
                tiles.append(
                    (
                        full[:, :128],
                        jnp.concatenate(
                            [full[:, 128:], jnp.zeros((ROWS, 128 - tail), jnp.float32)], axis=1
                        ),
                    )
                )
            height = mats.shape[1] // 2
            for i in range(per):
                base = pltpu.roll(tiles[i][0], lax.rem(128 - WIDTH * chip, 128), 1)
                base = jnp.where(beyond, pltpu.roll(tiles[i][1], 2, 1), base)
                base = jnp.where(lane < WIDTH, base, 0.0)
                base = base + pltpu.roll(base, WIDTH, 1) + pltpu.roll(base, 2 * WIDTH, 1)
                high = base.astype(jnp.bfloat16)
                low = (base - high.astype(jnp.float32)).astype(jnp.bfloat16)
                lanes = pl.ds(pl.multiple_of((q * per + i) * 128, 128), 128)
                replicas[pl.ds(at, ROWS), lanes] = high
                replicas[pl.ds(height + at, ROWS), lanes] = low
            for g in range(groups):
                which, at_lane = divmod(g * ROWS, 128)
                value = jnp.zeros((ROWS, 128), jnp.float32)
                for i in range(per):
                    shift = (i * ROWS - at_lane) % 128
                    piece = tiles[i][which]
                    if shift:
                        piece = pltpu.roll(piece, shift, 1)
                    value = jnp.where((lane >= i * ROWS) & (lane < (i + 1) * ROWS), piece, value)
                high = value.astype(jnp.bfloat16)
                low = (value - high.astype(jnp.float32)).astype(jnp.bfloat16)
                mats[g, pl.ds(at, ROWS), pl.ds(pl.multiple_of(q * 128, 128), 128)] = high
                mats[g, pl.ds(height + at, ROWS), pl.ds(pl.multiple_of(q * 128, 128), 128)] = low

        whole = coef // ROWS
        left = coef - whole * ROWS

        @pl.when(lax.rem(n, groups) < whole)
        def _():
            rows_at(lambda j: ops_ref[j, pl.ds(at, ROWS), :], at)

        @pl.when(lax.rem(n, groups) == whole)
        def _():
            rows_at(
                lambda j: jnp.concatenate(
                    [
                        ops_ref[j, whole * ROWS : coef, :],
                        jnp.zeros((ROWS - left, coef), jnp.float32),
                    ],
                    axis=0,
                ),
                whole * ROWS,
            )

    def multiply(g):
        halves = lanes_below((16, 8, 128), 64)

        def cut(c, carry):
            at = pl.multiple_of(c * 16, 16)
            block = table[g, pl.ds(at, 16)]
            high = block.astype(jnp.bfloat16).astype(jnp.float32)
            low = block - high
            top = jnp.where(halves, high, pltpu.roll(low, 64, 2))
            bottom = jnp.where(halves, pltpu.roll(high, 64, 2), low)
            split[pl.ds(at + 1, 16)] = jnp.concatenate([top, bottom], axis=1).astype(jnp.bfloat16)
            return carry

        known = (own + (steps - 1) * sent) // 16
        lax.fori_loop(0, known, cut, 0, unroll=True)
        receive(g, steps - 1)
        lax.fori_loop(known, known + sent // 16, cut, 0)
        height = mats.shape[1] // 2

        def targets(p, carry):
            sides = []
            for side in range(WIDE):
                sides.append(
                    jnp.concatenate(
                        [split[lists_ref[WIDE * p + side, j] + 1] for j in range(slots)], axis=0
                    )
                )
            source = jnp.concatenate(sides, axis=1)
            product = jnp.dot(mats[g], source, preferred_element_type=jnp.float32)
            lanes = pl.ds(pl.multiple_of(p * WIDE * 128, WIDE * 128), WIDE * 128)
            total[:, lanes] += product[:height] + product[height:]
            return carry

        lax.fori_loop(0, own // WIDE, targets, 0)

    lane = lax.broadcasted_iota(jnp.int32, (cells, 128), 1)
    part_of = jnp.where(lane < WIDTH, 0, jnp.where(lane < 2 * WIDTH, 1, jnp.where(lane < 3 * WIDTH, 2, 7)))

    def coarse_chunk(c):
        for i in range(CHUNK):
            def take(x, carry, i=i):
                for r in range(cells):
                    row = codes_smem[x, c * CHUNK + i, r]
                    gathered[i, pl.ds(pl.multiple_of(x * cells, 8) + r, 1), :] = everything[
                        pl.ds(row, 1), :
                    ]
                return carry

            lax.fori_loop(0, XCHIPS, take, 0)
        highs, lows = [], []
        for x in range(XCHIPS):
            turned = pltpu.roll(codes[x, slots : slots + cells, :], lax.rem(128 - c * CHUNK, 128), 1)
            row_high, row_low = [], []
            for i in range(CHUNK):
                value = gathered[i, x * cells : (x + 1) * cells]
                value = jnp.where(part_of == turned[:, i : i + 1], value, 0.0)
                high = value.astype(jnp.bfloat16)
                row_high.append(high)
                row_low.append((value - high.astype(jnp.float32)).astype(jnp.bfloat16))
            highs.append(jnp.concatenate(row_high, axis=1))
            lows.append(jnp.concatenate(row_low, axis=1))
        high = jnp.concatenate(highs, axis=0)
        low = jnp.concatenate(lows, axis=0)
        height = mats.shape[1] // 2
        lanes = pl.ds(pl.multiple_of(c * CHUNK * 128, CHUNK * 128), CHUNK * 128)
        op_high = replicas[:height, lanes]
        op_low = replicas[height:, lanes]
        dims = (((1,), (1,)), ((), ()))

        def dot(a, b):
            return lax.dot_general(a, b, dims, preferred_element_type=jnp.float32)

        product = dot(high, op_high) + dot(low, op_high) + dot(high, op_low)
        for x in range(XCHIPS):
            partial[x] += product[x * cells : (x + 1) * cells]

    for o in range(1, XCHIPS):
        slice_copy(o).start()
        code_copy(o).start()

    def tick(s, carry):
        for k in ORDER:
            late = s - offsets[k]
            g = late // STRIDES[k]

            @pl.when((late >= 0) & (g < groups) & (lax.rem(late, STRIDES[k]) == 0))
            def _():
                send(g, k)

        @pl.when(s == 0)
        def _():
            lax.fori_loop(0, slots, lambda j, c: (ops_copy(j).start(), c)[1], 0)
            total[...] = jnp.zeros_like(total)
            partial[...] = jnp.zeros_like(partial)

        @pl.when(s == X_TICK)
        def _():
            for o in range(1, XCHIPS):
                slice_copy(o).wait_recv()
            for o in range(1, 8):
                z_copy(o).start()

        @pl.when(s == Y_TICK)
        def _():
            for o in range(1, 8):
                z_copy(o).wait_recv()
            for o in range(1, 4):
                y_copy(o).start()

        @pl.when(s == CORE_TICK)
        def _():
            for o in range(1, 4):
                y_copy(o).wait_recv()
            core_copy().start()
            for o in range(1, XCHIPS):
                code_copy(o).wait_recv()
            codes_copy().start()

        @pl.when(s == ARRANGE_TICK)
        def _():
            lax.fori_loop(0, slots, lambda j, c: (ops_copy(j).wait(), c)[1], 0)

        first = (s - ARRANGE_TICK) * ARRANGE_STEP
        last = jnp.minimum(first + ARRANGE_STEP, groups * slots * ROWS // 128)

        @pl.when(first >= 0)
        def _():
            lax.fori_loop(first, last, lambda n, c: (arrange(n), c)[1], 0)

        @pl.when(s == COARSE_TICK)
        def _():
            core_copy().wait_recv()
            codes_copy().wait()

        @pl.when((s >= COARSE_TICK) & (s < COARSE_TICK + slots // CHUNK))
        def _():
            coarse_chunk(s - COARSE_TICK)

        @pl.when(s == COARSE_TICK + slots // CHUNK - 1)
        def _():
            for o in range(1, XCHIPS):
                sum_copy(o).start()

        late = s - offsets[steps]
        g = late // STRIDES[steps]

        @pl.when((late >= 0) & (g < groups) & (lax.rem(late, STRIDES[steps]) == 0))
        def _():
            multiply(g)

        return carry

    lax.fori_loop(0, (groups - 1) * STRIDES[steps] + offsets[steps] + 1, tick, 0)

    def drain(g, carry):
        for k in range(steps):
            copy(g, k).wait_send()
        return carry

    lax.fori_loop(0, groups - 1, drain, 0)
    for k in range(steps):
        copy(groups - 1, k, sent // 2).wait_send()

    for o in range(1, XCHIPS):
        sum_copy(o).wait_recv()
    coarse_out_ref[...] = (
        (partial[chip] + incoming[x_peer(1)]) + (incoming[x_peer(2)] + incoming[x_peer(3)])
    )[:, :coef]
    for o in range(1, XCHIPS):
        slice_copy(o).wait_send()
        code_copy(o).wait_send()
        sum_copy(o).wait_send()
        y_copy(o).wait_send()
    for o in range(1, 8):
        z_copy(o).wait_send()
    core_copy().wait_send()

    side = lanes_below((coef, 128), 64)

    def finish(p, carry):
        left = total[:coef, pl.ds(pl.multiple_of(p * 256, 256), 128)]
        right = total[:coef, pl.ds(pl.multiple_of(p * 256 + 128, 128), 128)]
        left = left + pltpu.roll(left, 64, 1)
        right = right + pltpu.roll(right, 64, 1)
        both = jnp.where(side, left, right)
        out_ref[:, pl.ds(pl.multiple_of(p * 128, 128), 128)] = both
        return carry

    lax.fori_loop(0, own // 2, finish, 0, unroll=4)


def source_codes(coarse_lists):
    cells, slots = coarse_lists.shape
    index = jnp.maximum(coarse_lists, 0)
    cell, device = index % cells, index // cells
    gy, gx = device % 32, device // 32
    place = (((gx % 2) * 4 + gy % 4) * 8 + gy // 4) * XCHIPS + gx // 2
    row = (place * PACKED + cell % PACKED).astype(jnp.int32)
    part = jnp.where(coarse_lists < 0, PARTS, cell // PACKED).astype(jnp.int32)
    by_slot = jnp.pad(row.T, ((0, 0), (0, 128 - cells)))
    by_cell = jnp.pad(part, ((0, 0), (0, 128 - slots)))
    return jnp.concatenate([by_slot, by_cell], axis=0)


def shards(multipoles, coarse_poles, operators, block_lists, coarse_lists, send_lists, live_blocks):
    coef, cells = multipoles.shape
    slots = operators.shape[0]
    coarse_cells = coarse_poles.shape[1]
    own = cells // BCELLS
    _, steps, sent = send_lists.shape
    groups = -(-coef // ROWS)
    height = groups * ROWS
    held = own + steps * sent
    low_bits = lax.axis_size("gy").bit_length() - 1
    offsets = OFFSETS
    vmem = pl.BlockSpec(memory_space=pltpu.VMEM)
    smem = pl.BlockSpec(memory_space=pltpu.SMEM)
    f32, bf16, dma = jnp.float32, jnp.bfloat16, pltpu.SemaphoreType.DMA
    fine_local, coarse_local = pl.pallas_call(
        functools.partial(fine_kernel, groups, steps, own, sent, low_bits, offsets),
        out_shape=(
            jax.ShapeDtypeStruct((coef, cells), f32),
            jax.ShapeDtypeStruct((coarse_cells, coef), f32),
        ),
        in_specs=[vmem, vmem, pl.BlockSpec(memory_space=pl.ANY), vmem, smem, smem],
        out_specs=(vmem, vmem),
        scratch_shapes=[
            pltpu.VMEM((groups, held, 8, 128), f32),
            pltpu.VMEM((groups, steps, sent, 8, 128), f32),
            pltpu.VMEM((groups, steps, sent, 8, 128), f32),
            pltpu.VMEM((held + 1, ROWS, 128), bf16),
            pltpu.VMEM((groups, 2 * height, slots * ROWS), bf16),
            pltpu.VMEM((height, own * 128), f32),
            pltpu.VMEM((slots, coef, coef), f32),
            pltpu.VMEM((XCHIPS, PACKED, 128), f32),
            pltpu.VMEM((64 * XCHIPS * PACKED, 128), f32),
            pltpu.VMEM((XCHIPS, slots + coarse_cells, 128), jnp.int32),
            pltpu.SMEM((XCHIPS, slots, 128), jnp.int32),
            pltpu.VMEM((2 * height, slots * 128), bf16),
            pltpu.VMEM((CHUNK, XCHIPS * coarse_cells, 128), f32),
            pltpu.VMEM((XCHIPS, coarse_cells, height), f32),
            pltpu.VMEM((XCHIPS, coarse_cells, height), f32),
            dma((groups, steps)),
            dma((groups, steps)),
            dma((slots,)),
            dma((XCHIPS - 1,)),
            dma((XCHIPS - 1,)),
            dma((XCHIPS - 1,)),
            dma((XCHIPS - 1,)),
            dma((7,)),
            dma((7,)),
            dma((3,)),
            dma((3,)),
            dma,
            dma,
            dma((XCHIPS - 1,)),
            dma((XCHIPS - 1,)),
            dma,
        ],
        compiler_params=pltpu.CompilerParams(
            collective_id=0, has_side_effects=True, vmem_limit_bytes=62 << 20
        ),
        cost_estimate=pl.CostEstimate(
            flops=8 * slots * coef * coef * cells, bytes_accessed=8 << 20, transcendentals=0
        ),
        name="far_field",
    )(
        multipoles,
        coarse_poles.T,
        operators.transpose(1, 0, 2),
        source_codes(coarse_lists),
        send_lists[0],
        block_lists,
    )
    inside = jnp.arange(cells, dtype=jnp.int32) < live_blocks[0] * BCELLS
    return (jnp.where(inside[None, :], fine_local, 0.0), coarse_local.T)


def solution(mesh):
    return jax.shard_map(
        shards,
        mesh=mesh,
        in_specs=(
            P(None, ("gx", "gy")),
            P(None, ("gx", "gy")),
            P(),
            P(("gx", "gy"), None),
            P(("gx", "gy"), None),
            P(("gx", "gy"), None, None),
            P(("gx", "gy")),
        ),
        out_specs=(P(None, ("gx", "gy")), P(None, ("gx", "gy"))),
        check_vma=False,
    )
```

```python
import functools
import jax
import jax.numpy as jnp
from jax import lax
from jax.experimental import pallas as pl
from jax.experimental.pallas import tpu as pltpu
from jax.sharding import PartitionSpec as P

BCELLS = 64
ROWS = 16
XCHIPS = 4
WIDTH = 42
PARTS = 3
PACKED = 24
CHUNK = 4
WIDE = 32
STRIDES = (1, 1, 1, 1, 1, 1, 1, 1, 1)
ORDER = (0, 1, 2, 3, 4, 5, 6, 7)
OFFSETS = (0, 1, 2, 3, 4, 6, 7, 8, 9)
X_TICK, Y_TICK, CORE_TICK, COARSE_TICK = 1, 5, 9, 11
ARRANGE_TICK, ARRANGE_STEP = 2, 6
MESH = pl.DeviceIdType.MESH


def lanes_below(shape, limit):
    return lax.broadcasted_iota(jnp.int32, shape, len(shape) - 1) < limit


def fine_kernel(
    groups, steps, own, sent, low_bits, offsets,
    mult_ref, coarse_ref, ops_hbm, codes_ref, send_ref, lists_ref,
    out_ref, coarse_out_ref,
    table, outgo, landed, split, mats, total, ops_ref,
    packed, everything, codes, codes_smem, replicas, gathered, partial, incoming,
    send_sem, recv_sem, ops_sem, slice_send, slice_recv, code_send, code_recv,
    z_send, z_recv, y_send, y_recv, core_send, core_recv, sum_send, sum_recv, smem_sem,
):
    slots, coef, _ = ops_ref.shape
    gx = lax.axis_index("gx")
    gy = lax.axis_index("gy")
    chip, core = gx // 2, lax.rem(gx, 2)
    z, y = gy // 4, lax.rem(gy, 4)
    cells = coarse_ref.shape[0]

    def x_peer(o):
        return lax.rem(chip + o, XCHIPS)

    def x_device(o):
        return (x_peer(o) * 2 + core, gy)

    def z_device(o):
        return (gx, lax.rem(z + o, 8) * 4 + y)

    def y_device(o):
        return (gx, z * 4 + lax.rem(y + o, 4))

    def core_device():
        return (gx + 1 - 2 * core, gy)

    def rows_of(c, yy, zz, xx, count):
        at = (((c * 4 + yy) * 8 + zz) * XCHIPS + xx) * PACKED
        return pl.ds(pl.multiple_of(at, 8), count * PACKED)

    def remote(source, target, send, recv, device):
        return pltpu.make_async_remote_copy(
            src_ref=source, dst_ref=target, send_sem=send, recv_sem=recv,
            device_id=device, device_id_type=MESH,
        )

    def slice_copy(o):
        return remote(
            packed.at[x_peer(o)], everything.at[rows_of(core, y, z, chip, 1)],
            slice_send.at[o - 1], slice_recv.at[o - 1], x_device(o),
        )

    def code_copy(o):
        return remote(
            codes_ref, codes.at[chip], code_send.at[o - 1], code_recv.at[o - 1], x_device(o)
        )

    def z_copy(o):
        rows = rows_of(core, y, z, 0, XCHIPS)
        return remote(
            everything.at[rows], everything.at[rows], z_send.at[o - 1], z_recv.at[o - 1], z_device(o)
        )

    def y_copy(o):
        rows = rows_of(core, y, 0, 0, 8 * XCHIPS)
        return remote(
            everything.at[rows], everything.at[rows], y_send.at[o - 1], y_recv.at[o - 1], y_device(o)
        )

    def core_copy():
        rows = rows_of(core, 0, 0, 0, 32 * XCHIPS)
        return remote(everything.at[rows], everything.at[rows], core_send, core_recv, core_device())

    def sum_copy(o):
        return remote(
            partial.at[x_peer(o)], incoming.at[chip],
            sum_send.at[o - 1], sum_recv.at[o - 1], x_device(o),
        )

    def ops_copy(j):
        return pltpu.make_async_copy(ops_hbm.at[:, j, :], ops_ref.at[j], ops_sem.at[j])

    def codes_copy():
        return pltpu.make_async_copy(codes.at[:, 0:slots], codes_smem, smem_sem)

    def partner(k):
        if k < low_bits:
            bit = 1 << k
            up = lax.rem(gy // bit, 2)
            return (gx, gy + bit - 2 * bit * up)
        bit = 1 << (k - low_bits)
        up = lax.rem(gx // bit, 2)
        return (gx + bit - 2 * bit * up, gy)

    def copy(g, k, count=sent):
        return pltpu.make_async_remote_copy(
            src_ref=outgo.at[g, k, pl.ds(0, count)],
            dst_ref=landed.at[g, k, pl.ds(0, count)],
            send_sem=send_sem.at[g, k],
            recv_sem=recv_sem.at[g, k],
            device_id=partner(k),
            device_id_type=MESH,
        )

    def receive(g, k):
        first = own + k * sent

        @pl.when(g < groups - 1)
        def _():
            copy(g, k).wait_recv()
            table[g, first : first + sent] = landed[g, k]

        @pl.when(g == groups - 1)
        def _():
            copy(g, k, sent // 2).wait_recv()
            for i in range(sent // 2):
                both = landed[g, k, i]
                table[g, first + i] = jnp.where(half, both, 0.0)
                table[g, first + sent // 2 + i] = jnp.where(half, pltpu.roll(both, 64, 1), 0.0)

    barrier = pltpu.get_barrier_semaphore()
    peers = [x_device(o) for o in range(1, XCHIPS)] + [z_device(o) for o in range(1, 8)]
    peers += [y_device(o) for o in range(1, 4)] + [core_device()]
    for peer in peers:
        pl.semaphore_signal(barrier, inc=1, device_id=peer, device_id_type=MESH)

    lane64 = lax.broadcasted_iota(jnp.int32, (cells, 128), 1)
    near = coarse_ref[:, :128]
    far = jnp.concatenate(
        [coarse_ref[:, 128:], jnp.zeros((cells, 256 - coef), jnp.float32)], axis=1
    )
    for x in range(XCHIPS):
        shift = (128 - WIDTH * x) % 128
        base = pltpu.roll(near, shift, 1) if shift else near
        if x == XCHIPS - 1:
            base = jnp.where(lane64 < shift, base, pltpu.roll(far, shift, 1))
        base = jnp.where(lane64 < WIDTH, base, 0.0)
        rest = jnp.concatenate(
            [base[2 * PACKED :], jnp.zeros((3 * PACKED - cells, 128), jnp.float32)], axis=0
        )
        packed[x] = (
            base[:PACKED]
            + pltpu.roll(base[PACKED : 2 * PACKED], WIDTH, 1)
            + pltpu.roll(rest, 2 * WIDTH, 1)
        )
    everything[rows_of(core, y, z, chip, 1)] = packed[chip]
    codes[chip] = codes_ref[...]

    half = lanes_below((8, 128), 64)

    def place(g, p, first, second):
        table[g, 2 * p] = jnp.where(half, first, pltpu.roll(second, 64, 1))
        table[g, 2 * p + 1] = jnp.where(half, pltpu.roll(first, 64, 1), second)

    def own_blocks(g):
        def pair(p, c):
            lanes = pl.ds(pl.multiple_of(p * 128, 128), 128)
            first = mult_ref[pl.ds(pl.multiple_of(g * ROWS, 8), 8), lanes]
            second = mult_ref[pl.ds(pl.multiple_of(g * ROWS + 8, 8), 8), lanes]
            place(g, p, first, second)
            return c

        lax.fori_loop(0, own // 2, pair, 0, unroll=True)

    def last_blocks():
        g = groups - 1
        left = coef - g * ROWS

        def pair(p, c):
            lanes = pl.ds(pl.multiple_of(p * 128, 128), 128)
            first = jnp.concatenate(
                [mult_ref[g * ROWS : coef, lanes], jnp.zeros((8 - left, 128), jnp.float32)], axis=0
            )
            place(g, p, first, jnp.zeros((8, 128), jnp.float32))
            return c

        lax.fori_loop(0, own // 2, pair, 0)

    split[0] = jnp.zeros((ROWS, 128), jnp.bfloat16)
    pl.semaphore_wait(barrier, len(peers))

    def send(g, k):
        if k == 0:

            @pl.when(g < groups - 1)
            def _():
                own_blocks(g)

            @pl.when(g == groups - 1)
            def _():
                last_blocks()

        if k > 0:
            receive(g, k - 1)

        @pl.when(g < groups - 1)
        def _():
            for i in range(sent):
                outgo[g, k, i] = table[g, send_ref[k, i]]
            copy(g, k).start()

        @pl.when(g == groups - 1)
        def _():
            for i in range(sent // 2):
                other = pltpu.roll(table[g, send_ref[k, sent // 2 + i]], 64, 1)
                outgo[g, k, i] = jnp.where(half, table[g, send_ref[k, i]], other)
            copy(g, k, sent // 2).start()

    def arrange(n):
        q, at = n // groups, pl.multiple_of(lax.rem(n, groups) * ROWS, ROWS)
        per = 128 // ROWS
        lane = lax.broadcasted_iota(jnp.int32, (ROWS, 128), 1)
        tail = coef - 128
        beyond = (lane >= 2) & (jnp.full((ROWS, 128), chip, jnp.int32) == XCHIPS - 1)

        def rows_at(read, at):
            tiles = []
            for i in range(per):
                full = read(q * per + i)
                tiles.append(
                    (
                        full[:, :128],
                        jnp.concatenate(
                            [full[:, 128:], jnp.zeros((ROWS, 128 - tail), jnp.float32)], axis=1
                        ),
                    )
                )
            height = mats.shape[1] // 2
            for i in range(per):
                base = pltpu.roll(tiles[i][0], lax.rem(128 - WIDTH * chip, 128), 1)
                base = jnp.where(beyond, pltpu.roll(tiles[i][1], 2, 1), base)
                base = jnp.where(lane < WIDTH, base, 0.0)
                base = base + pltpu.roll(base, WIDTH, 1) + pltpu.roll(base, 2 * WIDTH, 1)
                high = base.astype(jnp.bfloat16)
                low = (base - high.astype(jnp.float32)).astype(jnp.bfloat16)
                lanes = pl.ds(pl.multiple_of((q * per + i) * 128, 128), 128)
                replicas[pl.ds(at, ROWS), lanes] = high
                replicas[pl.ds(height + at, ROWS), lanes] = low
            for g in range(groups):
                which, at_lane = divmod(g * ROWS, 128)
                value = jnp.zeros((ROWS, 128), jnp.float32)
                for i in range(per):
                    shift = (i * ROWS - at_lane) % 128
                    piece = tiles[i][which]
                    if shift:
                        piece = pltpu.roll(piece, shift, 1)
                    value = jnp.where((lane >= i * ROWS) & (lane < (i + 1) * ROWS), piece, value)
                high = value.astype(jnp.bfloat16)
                low = (value - high.astype(jnp.float32)).astype(jnp.bfloat16)
                mats[g, pl.ds(at, ROWS), pl.ds(pl.multiple_of(q * 128, 128), 128)] = high
                mats[g, pl.ds(height + at, ROWS), pl.ds(pl.multiple_of(q * 128, 128), 128)] = low

        whole = coef // ROWS
        left = coef - whole * ROWS

        @pl.when(lax.rem(n, groups) < whole)
        def _():
            rows_at(lambda j: ops_ref[j, pl.ds(at, ROWS), :], at)

        @pl.when(lax.rem(n, groups) == whole)
        def _():
            rows_at(
                lambda j: jnp.concatenate(
                    [
                        ops_ref[j, whole * ROWS : coef, :],
                        jnp.zeros((ROWS - left, coef), jnp.float32),
                    ],
                    axis=0,
                ),
                whole * ROWS,
            )

    def multiply(g):
        halves = lanes_below((16, 8, 128), 64)

        def cut(c, carry):
            at = pl.multiple_of(c * 16, 16)
            block = table[g, pl.ds(at, 16)]
            high = block.astype(jnp.bfloat16).astype(jnp.float32)
            low = block - high
            top = jnp.where(halves, high, pltpu.roll(low, 64, 2))
            bottom = jnp.where(halves, pltpu.roll(high, 64, 2), low)
            split[pl.ds(at + 1, 16)] = jnp.concatenate([top, bottom], axis=1).astype(jnp.bfloat16)
            return carry

        known = (own + (steps - 1) * sent) // 16
        lax.fori_loop(0, known, cut, 0, unroll=True)
        receive(g, steps - 1)
        lax.fori_loop(known, known + sent // 16, cut, 0)
        height = mats.shape[1] // 2

        def targets(p, carry):
            sides = []
            for side in range(WIDE):
                sides.append(
                    jnp.concatenate(
                        [split[lists_ref[WIDE * p + side, j] + 1] for j in range(slots)], axis=0
                    )
                )
            source = jnp.concatenate(sides, axis=1)
            product = jnp.dot(mats[g], source, preferred_element_type=jnp.float32)
            lanes = pl.ds(pl.multiple_of(p * WIDE * 128, WIDE * 128), WIDE * 128)
            total[:, lanes] += product[:height] + product[height:]
            return carry

        lax.fori_loop(0, own // WIDE, targets, 0)

    lane = lax.broadcasted_iota(jnp.int32, (cells, 128), 1)
    part_of = jnp.where(lane < WIDTH, 0, jnp.where(lane < 2 * WIDTH, 1, jnp.where(lane < 3 * WIDTH, 2, 7)))

    def coarse_chunk(c):
        for i in range(CHUNK):
            def take(x, carry, i=i):
                for r in range(cells):
                    row = codes_smem[x, c * CHUNK + i, r]
                    gathered[i, pl.ds(pl.multiple_of(x * cells, 8) + r, 1), :] = everything[
                        pl.ds(row, 1), :
                    ]
                return carry

            lax.fori_loop(0, XCHIPS, take, 0)
        highs, lows = [], []
        for x in range(XCHIPS):
            turned = pltpu.roll(codes[x, slots : slots + cells, :], lax.rem(128 - c * CHUNK, 128), 1)
            row_high, row_low = [], []
            for i in range(CHUNK):
                value = gathered[i, x * cells : (x + 1) * cells]
                value = jnp.where(part_of == turned[:, i : i + 1], value, 0.0)
                high = value.astype(jnp.bfloat16)
                row_high.append(high)
                row_low.append((value - high.astype(jnp.float32)).astype(jnp.bfloat16))
            highs.append(jnp.concatenate(row_high, axis=1))
            lows.append(jnp.concatenate(row_low, axis=1))
        high = jnp.concatenate(highs, axis=0)
        low = jnp.concatenate(lows, axis=0)
        height = mats.shape[1] // 2
        lanes = pl.ds(pl.multiple_of(c * CHUNK * 128, CHUNK * 128), CHUNK * 128)
        op_high = replicas[:height, lanes]
        op_low = replicas[height:, lanes]
        dims = (((1,), (1,)), ((), ()))

        def dot(a, b):
            return lax.dot_general(a, b, dims, preferred_element_type=jnp.float32)

        product = dot(high, op_high) + dot(low, op_high) + dot(high, op_low)
        for x in range(XCHIPS):
            partial[x] += product[x * cells : (x + 1) * cells]

    for o in range(1, XCHIPS):
        slice_copy(o).start()
        code_copy(o).start()

    def tick(s, carry):
        for k in ORDER:
            late = s - offsets[k]
            g = late // STRIDES[k]

            @pl.when((late >= 0) & (g < groups) & (lax.rem(late, STRIDES[k]) == 0))
            def _():
                send(g, k)

        @pl.when(s == 0)
        def _():
            lax.fori_loop(0, slots, lambda j, c: (ops_copy(j).start(), c)[1], 0)
            total[...] = jnp.zeros_like(total)
            partial[...] = jnp.zeros_like(partial)

        @pl.when(s == X_TICK)
        def _():
            for o in range(1, XCHIPS):
                slice_copy(o).wait_recv()
            for o in range(1, 8):
                z_copy(o).start()

        @pl.when(s == Y_TICK)
        def _():
            for o in range(1, 8):
                z_copy(o).wait_recv()
            for o in range(1, 4):
                y_copy(o).start()

        @pl.when(s == CORE_TICK)
        def _():
            for o in range(1, 4):
                y_copy(o).wait_recv()
            core_copy().start()
            for o in range(1, XCHIPS):
                code_copy(o).wait_recv()
            codes_copy().start()

        @pl.when(s == ARRANGE_TICK)
        def _():
            lax.fori_loop(0, slots, lambda j, c: (ops_copy(j).wait(), c)[1], 0)

        first = (s - ARRANGE_TICK) * ARRANGE_STEP
        last = jnp.minimum(first + ARRANGE_STEP, groups * slots * ROWS // 128)

        @pl.when(first >= 0)
        def _():
            lax.fori_loop(first, last, lambda n, c: (arrange(n), c)[1], 0)

        @pl.when(s == COARSE_TICK)
        def _():
            core_copy().wait_recv()
            codes_copy().wait()

        @pl.when((s >= COARSE_TICK) & (s < COARSE_TICK + slots // CHUNK))
        def _():
            coarse_chunk(s - COARSE_TICK)

        @pl.when(s == COARSE_TICK + slots // CHUNK - 1)
        def _():
            for o in range(1, XCHIPS):
                sum_copy(o).start()

        late = s - offsets[steps]
        g = late // STRIDES[steps]

        @pl.when((late >= 0) & (g < groups) & (lax.rem(late, STRIDES[steps]) == 0))
        def _():
            multiply(g)

        return carry

    lax.fori_loop(0, (groups - 1) * STRIDES[steps] + offsets[steps] + 1, tick, 0)

    def drain(g, carry):
        for k in range(steps):
            copy(g, k).wait_send()
        return carry

    lax.fori_loop(0, groups - 1, drain, 0)
    for k in range(steps):
        copy(groups - 1, k, sent // 2).wait_send()

    for o in range(1, XCHIPS):
        sum_copy(o).wait_recv()
    coarse_out_ref[...] = (
        (partial[chip] + incoming[x_peer(1)]) + (incoming[x_peer(2)] + incoming[x_peer(3)])
    )[:, :coef]
    for o in range(1, XCHIPS):
        slice_copy(o).wait_send()
        code_copy(o).wait_send()
        sum_copy(o).wait_send()
        y_copy(o).wait_send()
    for o in range(1, 8):
        z_copy(o).wait_send()
    core_copy().wait_send()

    side = lanes_below((coef, 128), 64)

    def finish(p, carry):
        left = total[:coef, pl.ds(pl.multiple_of(p * 256, 256), 128)]
        right = total[:coef, pl.ds(pl.multiple_of(p * 256 + 128, 128), 128)]
        left = left + pltpu.roll(left, 64, 1)
        right = right + pltpu.roll(right, 64, 1)
        both = jnp.where(side, left, right)
        out_ref[:, pl.ds(pl.multiple_of(p * 128, 128), 128)] = both
        return carry

    lax.fori_loop(0, own // 2, finish, 0, unroll=4)


def source_codes(coarse_lists):
    cells, slots = coarse_lists.shape
    index = jnp.maximum(coarse_lists, 0)
    cell, device = index % cells, index // cells
    gy, gx = device % 32, device // 32
    place = (((gx % 2) * 4 + gy % 4) * 8 + gy // 4) * XCHIPS + gx // 2
    row = (place * PACKED + cell % PACKED).astype(jnp.int32)
    part = jnp.where(coarse_lists < 0, PARTS, cell // PACKED).astype(jnp.int32)
    by_slot = jnp.pad(row.T, ((0, 0), (0, 128 - cells)))
    by_cell = jnp.pad(part, ((0, 0), (0, 128 - slots)))
    return jnp.concatenate([by_slot, by_cell], axis=0)


def shards(multipoles, coarse_poles, operators, block_lists, coarse_lists, send_lists, live_blocks):
    coef, cells = multipoles.shape
    slots = operators.shape[0]
    coarse_cells = coarse_poles.shape[1]
    own = cells // BCELLS
    _, steps, sent = send_lists.shape
    groups = -(-coef // ROWS)
    height = groups * ROWS
    held = own + steps * sent
    low_bits = lax.axis_size("gy").bit_length() - 1
    offsets = OFFSETS
    vmem = pl.BlockSpec(memory_space=pltpu.VMEM)
    smem = pl.BlockSpec(memory_space=pltpu.SMEM)
    f32, bf16, dma = jnp.float32, jnp.bfloat16, pltpu.SemaphoreType.DMA
    fine_local, coarse_local = pl.pallas_call(
        functools.partial(fine_kernel, groups, steps, own, sent, low_bits, offsets),
        out_shape=(
            jax.ShapeDtypeStruct((coef, cells), f32),
            jax.ShapeDtypeStruct((coarse_cells, coef), f32),
        ),
        in_specs=[vmem, vmem, pl.BlockSpec(memory_space=pl.ANY), vmem, smem, smem],
        out_specs=(vmem, vmem),
        scratch_shapes=[
            pltpu.VMEM((groups, held, 8, 128), f32),
            pltpu.VMEM((groups, steps, sent, 8, 128), f32),
            pltpu.VMEM((groups, steps, sent, 8, 128), f32),
            pltpu.VMEM((held + 1, ROWS, 128), bf16),
            pltpu.VMEM((groups, 2 * height, slots * ROWS), bf16),
            pltpu.VMEM((height, own * 128), f32),
            pltpu.VMEM((slots, coef, coef), f32),
            pltpu.VMEM((XCHIPS, PACKED, 128), f32),
            pltpu.VMEM((64 * XCHIPS * PACKED, 128), f32),
            pltpu.VMEM((XCHIPS, slots + coarse_cells, 128), jnp.int32),
            pltpu.SMEM((XCHIPS, slots, 128), jnp.int32),
            pltpu.VMEM((2 * height, slots * 128), bf16),
            pltpu.VMEM((CHUNK, XCHIPS * coarse_cells, 128), f32),
            pltpu.VMEM((XCHIPS, coarse_cells, height), f32),
            pltpu.VMEM((XCHIPS, coarse_cells, height), f32),
            dma((groups, steps)),
            dma((groups, steps)),
            dma((slots,)),
            dma((XCHIPS - 1,)),
            dma((XCHIPS - 1,)),
            dma((XCHIPS - 1,)),
            dma((XCHIPS - 1,)),
            dma((7,)),
            dma((7,)),
            dma((3,)),
            dma((3,)),
            dma,
            dma,
            dma((XCHIPS - 1,)),
            dma((XCHIPS - 1,)),
            dma,
        ],
        compiler_params=pltpu.CompilerParams(
            collective_id=0, has_side_effects=True, vmem_limit_bytes=62 << 20
        ),
        cost_estimate=pl.CostEstimate(
            flops=8 * slots * coef * coef * cells, bytes_accessed=8 << 20, transcendentals=0
        ),
        name="far_field",
    )(
        multipoles,
        coarse_poles.T,
        operators.transpose(1, 0, 2),
        source_codes(coarse_lists),
        send_lists[0],
        block_lists,
    )
    inside = jnp.arange(cells, dtype=jnp.int32) < live_blocks[0] * BCELLS
    return (jnp.where(inside[None, :], fine_local, 0.0), coarse_local.T)


def solution(mesh):
    return jax.shard_map(
        shards,
        mesh=mesh,
        in_specs=(
            P(None, ("gx", "gy")),
            P(None, ("gx", "gy")),
            P(),
            P(("gx", "gy"), None),
            P(("gx", "gy"), None),
            P(("gx", "gy"), None, None),
            P(("gx", "gy")),
        ),
        out_specs=(P(None, ("gx", "gy")), P(None, ("gx", "gy"))),
        check_vma=False,
    )
```
